128 devices in a mesh: seq: 32 (over x, z_hi, y), head: 4 (over z_lo, core).
Axes of the slice: x: 4, y: 4, z: 4 (z_hi: 2, z_lo: 2; z = z_hi * 2 + z_lo), core: 2. Of those that a mesh axis runs over, the one named last changes fastest.
Arguments:
- residual_in: bfloat16 [4096, 4096], P(('seq', 'head')), may hold values from -3 to 3
- expert_hidden: bfloat16 [128, 128, 3, 1536], P(('seq', 'head')), may hold values from -6 to 6
- w_down: bfloat16 [128, 1536, 4096], P(('seq', 'head')), may hold values from -0.15625 to 0.15625
- routes: int32 [4096, 8], P(('seq', 'head')), may hold values from 0 to 127, all different within a row; in each aligned block of 32 rows (0 to 31, 32 to 63, ...) at most 3 rows name the same one
- gates: float32 [4096, 8], P(('seq', 'head')), may hold values from 0.05 to 0.3
- norm_gain: float32 [4096], replicated, may hold values from 0.1 to 1.9
- w_qkv: bfloat16 [4096, 4, 2304], P('seq', 'head'), may hold values from -0.09375 to 0.09375
- cache_kv: bfloat16 [12288, 4, 2, 128], P('seq', 'head'), may hold values from -600 to 600, as said below
Outputs:
- stream: bfloat16 [4096, 4096], P(('seq', 'head'))
- attended: bfloat16 [4096, 4, 2048], P('seq', 'head')
The draws below stay inside these ranges and needn't reach their ends.
Inputs may be any that keep to these rules, and one draw needn't show every extreme that they name: `routes`: each token names 8 different experts. Among the 32 tokens of one owner no expert is named by more than 3 tokens, and in some owners one expert is named by exactly 3. `cache_kv`: cached keys already carry their rotary phase for positions 0 to 12287.
All inputs are finite; a program needn't handle non-finite values.
Results may differ from the reference program's by a relative error of at most 0.024.
The reference program's roundings to bfloat16 on the way count: a program that leaves them out, or rounds other values in their place, can miss the bound.
Values may be sent and summed in bfloat16 or wider, within the bound.
No kernel may reach another device: no remote copies, remote signals or barrier semaphores. Data moves between devices by JAX's collectives and lax.ppermute only.
A program may use at most 320 MiB of HBM per device.

```python
import math
import jax
import jax.numpy as jnp
import numpy as np
from jax import lax

D = 4096
FF = 1536
TOP = 8
KVH = 4
QPK = 16
HD = 128
TOK_DEV = 32
EXPERTS = 128
OWNERS = 128
CAP = 3
TOKENS = 4096
CACHE = 12288
QKV = 2304


def draw_cache_kv(key, part):
    key = jax.random.fold_in(key, 7)
    base_key = jax.random.fold_in(key, 0)
    values = jnp.clip(jax.random.normal(base_key, (CACHE, KVH, 2, HD), jnp.float32), -6.0, 6.0)
    return values.astype(jnp.bfloat16)


def shard_levels(rng, shape, cuts, low, largest):
    def one(position, parts):
        steps = jax.random.uniform(jax.random.fold_in(jax.random.fold_in(rng, 6), position), (parts,), jnp.float32, low / len(cuts), largest / len(cuts))
        return jnp.repeat(jnp.exp(steps), shape[position] // parts).reshape((-1,) + (1,) * (len(shape) - position - 1))

    loudness = one(*cuts[0])
    for cut in cuts[1:]:
        loudness = loudness * one(*cut)
    return loudness


def routed_block(key, own, number, rows, count, top, bound, slope):
    order = jax.random.permutation(key, count)
    packed, common = load_shares(count, rows * top, bound, slope, True), load_shares(count, rows * top, bound, slope, False)
    places = jnp.arange(count)

    def named(lengths, offset_by):
        used = int((lengths > 0).sum())
        fixed = max(1, used // 4)
        moved = fixed + (places - fixed + offset_by * (used - fixed)) % max(1, count - fixed)
        return jnp.zeros((count,), jnp.int32).at[order[jnp.where(places < fixed, places, moved)]].set(jnp.asarray(lengths, jnp.int32))

    lengths = jnp.where(number % 4 == 0, named(packed, number // 4), named(common, number - number // 4 - 1))
    mixed = jax.random.permutation(jax.random.fold_in(own, 3), count)
    giver, sink = mixed[0:count // 2 * 2:2], mixed[1:count // 2 * 2:2]
    room = jnp.minimum(lengths[giver] - 1, bound - lengths[sink]) // 2
    room = jnp.where((giver == order[0]) | (sink == order[0]) | (lengths[sink] == 0), 0, jnp.maximum(room, 0))
    moved = jax.random.randint(jax.random.fold_in(own, 4), (count // 2,), 0, 1 << 20) % (room + 1)
    lengths = lengths.at[giver].add(-moved).at[sink].add(moved)
    items = jnp.searchsorted(jnp.cumsum(lengths), jnp.arange(rows * top), side="right").astype(jnp.int32)
    grid = items.reshape(top, rows).T
    grid = grid[jax.random.permutation(jax.random.fold_in(own, 1), rows)]
    offset_by = jax.random.randint(jax.random.fold_in(own, 2), (rows, 1), 0, top)
    return jnp.take_along_axis(grid, (jnp.arange(top)[None, :] + offset_by) % top, axis=1)


def load_shares(amount, total, reach, skew, full):
    portions = [(1 << 20) // math.isqrt(standing ** skew) + 1 for standing in range(1, amount + 1)]
    largest = reach if full else min(reach, max(-(-total // amount), total * portions[0] // sum(portions)))
    least = 1 if total - largest >= amount - 1 else 0
    holding, spare = [largest] + [least] * (amount - 1), total - largest - least * (amount - 1)
    while spare > 0:
        movable = [i for i in range(1, amount) if holding[i] < largest] or [i for i in range(1, amount) if holding[i] < reach]
        mass, remaining = sum([portions[i] for i in movable]), spare
        for i in movable:
            extra = min(reach - holding[i], max(1, remaining * portions[i] // mass), spare)
            holding[i] = holding[i] + extra
            spare = spare - extra
    return np.array(holding)


def bell_draw(key, shape, deviation, most, cuts=(), held_as=jnp.bfloat16):
    entries = jax.random.normal(key, shape, jnp.float32) * deviation
    if len(cuts) > 0:
        entries = shard_levels(key, shape, cuts, -0.22, 0.18) * entries
    return jnp.clip(entries, min=-most, max=most).astype(held_as)


def setup_inputs(seed: int = 0) -> dict:
    splits = jax.random.split(jax.random.key(seed), 9)
    residual_in = bell_draw(splits[0], (TOKENS, D), 0.5, 3.0, ((0, 128),))
    expert_hidden = bell_draw(splits[1], (EXPERTS, OWNERS, CAP, FF), 1.0, 6.0, ((0, 128),))
    w_down = bell_draw(splits[2], (EXPERTS, FF, D), FF ** -0.5, 0.15625, ((0, 128),))
    routes_keys = jax.random.split(jax.random.fold_in(splits[3], 1), TOKENS // TOK_DEV)
    routes_turns = jax.random.permutation(jax.random.fold_in(splits[3], 3), TOKENS // TOK_DEV)
    routes = jax.vmap(lambda own, number: routed_block(jax.random.fold_in(splits[3], 2), own, number, TOK_DEV, EXPERTS, TOP, CAP, 2))(routes_keys, routes_turns).reshape((TOKENS, TOP))
    gates = jnp.clip(0.05 + 0.25 * jax.random.uniform(splits[4], (TOKENS, TOP), jnp.float32) ** shard_levels(splits[4], (TOKENS, TOP), ((0, 128),), -0.2, 0.2), 0.05, 0.3)
    norm_gain = jnp.clip(1.0 + 0.18 * jax.random.normal(splits[5], (D,), jnp.float32), 0.1, 1.9)
    w_qkv = bell_draw(splits[6], (D, KVH, QKV), D ** -0.5, 0.09375, ((0, 32), (1, 4)))
    cache_kv = draw_cache_kv(jax.random.fold_in(splits[8], 71), 0)
    return {"residual_in": residual_in, "expert_hidden": expert_hidden, "w_down": w_down, "routes": routes, "gates": gates, "norm_gain": norm_gain, "w_qkv": w_qkv, "cache_kv": cache_kv}


rope_base = 1000000.0
masked_score = -1e+30

def slot_numbers(route_block):
    flat_routes = route_block.reshape(-1)
    per_token = route_block.shape[1]
    token_of = jnp.arange(flat_routes.shape[0], dtype=jnp.int32) // per_token
    earlier = (flat_routes[:, None] == flat_routes[None, :]) & (token_of[None, :] < token_of[:, None])
    return lax.optimization_barrier(jnp.sum(earlier.astype(jnp.int32), axis=1)).reshape(route_block.shape)

def rotate(values, positions):
    half_dim = values.shape[-1] // 2
    inverse = rope_base ** (-2.0 * jnp.arange(half_dim, dtype=jnp.float32) / values.shape[-1])
    angles = positions[:, None] * inverse[None, :]
    cosine = jnp.cos(angles)[:, None, :]
    sine_part = jnp.sin(angles)[:, None, :]
    first_half = values[..., :half_dim]
    second_half = values[..., half_dim:]
    return jnp.concatenate([first_half * cosine - second_half * sine_part, second_half * cosine + first_half * sine_part], axis=-1)

def reference(residual_in, expert_hidden, w_down, routes, gates, norm_gain, w_qkv, cache_kv):

    def expert_rows(pair):
        hidden_rows, weight = pair
        flat_hidden = hidden_rows.reshape(-1, FF).astype(jnp.float32)
        return jnp.dot(flat_hidden, weight.astype(jnp.float32)).astype(jnp.bfloat16)
    produced = lax.optimization_barrier(lax.map(expert_rows, (expert_hidden, w_down)))
    route_blocks = routes.reshape(OWNERS, TOK_DEV, TOP)
    slots_all = jax.vmap(slot_numbers)(route_blocks)
    owner_ids = jnp.arange(OWNERS, dtype=jnp.int32)[:, None, None]
    picked = produced[route_blocks, owner_ids * CAP + slots_all]
    moe_out = lax.optimization_barrier(jnp.sum(gates.reshape(OWNERS, TOK_DEV, TOP, 1) * picked.astype(jnp.float32), axis=2)).reshape(TOKENS, D)
    stream = (residual_in.astype(jnp.float32) + moe_out).astype(jnp.bfloat16)
    widened = lax.optimization_barrier(stream).astype(jnp.float32)
    inverse_rms = lax.rsqrt(lax.optimization_barrier(jnp.mean(widened * widened, axis=1, keepdims=True)) + 1e-06)
    normed = lax.optimization_barrier((widened * inverse_rms * norm_gain[None, :]).astype(jnp.bfloat16))
    projected = jnp.dot(normed.astype(jnp.float32), w_qkv.reshape(D, KVH * QKV).astype(jnp.float32))
    projected = projected.reshape(TOKENS, KVH, QPK + 2, HD)
    positions = (CACHE + jnp.arange(TOKENS, dtype=jnp.int32)).astype(jnp.float32)
    queries = rotate(projected[:, :, :QPK].reshape(TOKENS, KVH * QPK, HD), positions).astype(jnp.bfloat16)
    new_keys = rotate(projected[:, :, QPK], positions).astype(jnp.bfloat16)
    new_values = projected[:, :, QPK + 1].astype(jnp.bfloat16)
    queries, new_keys, new_values = lax.optimization_barrier((queries, new_keys, new_values))
    all_keys = jnp.concatenate([cache_kv[:, :, 0], new_keys], axis=0).transpose(1, 0, 2)
    all_values = jnp.concatenate([cache_kv[:, :, 1], new_values], axis=0).transpose(1, 0, 2)
    block_len = math.gcd(TOKENS, 256)
    block_total = TOKENS // block_len
    key_span = jnp.arange(CACHE + TOKENS, dtype=jnp.int32) - CACHE
    grouped = queries.reshape(block_total, block_len, KVH, QPK, HD).transpose(2, 0, 1, 3, 4)

    def per_head(head_args):
        head_queries, head_keys, head_values = head_args
        keys_wide = head_keys.astype(jnp.float32)
        values_wide = head_values.astype(jnp.float32)

        def per_block(block_args):
            block_queries, block_number = block_args
            query_span = block_number * block_len + jnp.arange(block_len, dtype=jnp.int32)
            rows_wide = block_queries.reshape(block_len * QPK, HD).astype(jnp.float32)
            scores = jnp.dot(rows_wide, keys_wide.T) * HD ** (-0.5)
            allowed = key_span[None, :] <= jnp.repeat(query_span, QPK)[:, None]
            scores = jnp.where(allowed, scores, masked_score)
            highest = lax.optimization_barrier(jnp.max(scores, axis=1))
            weights = jnp.where(allowed, jnp.exp(scores - highest[:, None]), 0.0)
            rounded = lax.optimization_barrier(weights.astype(jnp.bfloat16)).astype(jnp.float32)
            result = jnp.dot(rounded, values_wide) / lax.optimization_barrier(jnp.sum(weights, axis=1))[:, None]
            return result.astype(jnp.bfloat16).reshape(block_len, QPK * HD)
        return lax.map(per_block, (head_queries, jnp.arange(block_total, dtype=jnp.int32)))
    attended = lax.map(per_head, (grouped, all_keys, all_values))
    attended = attended.transpose(1, 2, 0, 3).reshape(TOKENS, KVH, QPK * HD)
    return (stream, attended)
```

```python
import functools

import jax
import jax.numpy as jnp
from jax import lax
from jax.experimental import pallas as pl
from jax.experimental.pallas import tpu as pltpu
from jax.sharding import Mesh, PartitionSpec as P

rope_base = 1000000.0
masked_score = -1e30
log2_e = 1.4426950408889634

token_axes = ("x", "zh", "y", "zl", "c")
seq_axes = ("x", "zh", "y")
head_axes = ("zl", "c")

MIB = 2**20
column_parts = 8


def slot_numbers(route_block):
    flat_routes = route_block.reshape(-1)
    per_token = route_block.shape[1]
    token_of = jnp.arange(flat_routes.shape[0], dtype=jnp.int32) // per_token
    earlier = (flat_routes[:, None] == flat_routes[None, :]) & (
        token_of[None, :] < token_of[:, None]
    )
    return jnp.sum(earlier.astype(jnp.int32), axis=1).reshape(route_block.shape)


def expert_kernel(x_ref, w_ref, o_ref, scratch):
    step = pl.program_id(0)
    rows = x_ref.shape[0]
    product = jnp.dot(x_ref[...], w_ref[...], preferred_element_type=jnp.float32)
    for lane in range(product.shape[1] // 128):
        scratch[lane, pl.ds(step, rows, stride=column_parts), :] = product[
            :, lane * 128 : (lane + 1) * 128
        ]

    @pl.when(step == column_parts - 1)
    def _():
        for lane in range(product.shape[1] // 128):
            o_ref[:, lane * 128 : (lane + 1) * 128] = scratch[lane].astype(jnp.bfloat16)


def expert_rows(hidden, weight):
    rows, depth = hidden.shape
    width = weight.shape[1]
    part = width // column_parts
    return pl.pallas_call(
        expert_kernel,
        grid=(column_parts,),
        in_specs=[
            pl.BlockSpec((rows, depth), lambda b: (0, 0)),
            pl.BlockSpec((depth, part), lambda b: (0, b)),
        ],
        out_specs=pl.BlockSpec((rows * column_parts, part), lambda b: (0, 0)),
        out_shape=jax.ShapeDtypeStruct((rows * column_parts, part), jnp.bfloat16),
        scratch_shapes=[pltpu.VMEM((part // 128, rows * column_parts, 128), jnp.float32)],
        compiler_params=pltpu.CompilerParams(vmem_limit_bytes=40 * MIB),
        cost_estimate=pl.CostEstimate(
            flops=2 * rows * depth * width,
            bytes_accessed=2 * (depth * width + rows * (depth + width)),
            transcendentals=0,
        ),
    )(hidden, weight)


def combine_kernel(row_ref, gate_ref, got_ref, res_ref, gain_ref, stream_ref, normed_ref, scratch):
    tokens, width = res_ref.shape
    per_token = row_ref.shape[0] // tokens
    part = got_ref.shape[2]

    def one(t, carry):
        total = jnp.zeros((column_parts, part), jnp.float32)
        for k in range(per_token):
            at = t * per_token + k
            total = total + gate_ref[at] * got_ref[row_ref[at]].astype(jnp.float32)
        first = pl.multiple_of(t * column_parts, column_parts)
        for lane in range(part // 128):
            scratch[lane, pl.ds(first, column_parts), :] = total[:, lane * 128 : (lane + 1) * 128]
        return carry

    lax.fori_loop(0, tokens, one, 0)
    squares = jnp.zeros((tokens, 128), jnp.float32)
    for b in range(column_parts):
        for lane in range(part // 128):
            cols = pl.ds(b * part + lane * 128, 128)
            moe = scratch[lane, pl.ds(b, tokens, stride=column_parts), :]
            stream = (res_ref[:, cols].astype(jnp.float32) + moe).astype(jnp.bfloat16)
            stream_ref[:, cols] = stream
            widened = stream.astype(jnp.float32)
            squares = squares + widened * widened
    mean = jnp.sum(squares, axis=1, keepdims=True) * (1.0 / width)
    inverse_rms = lax.rsqrt(mean + 1e-06)
    for b in range(width // 512):
        cols = pl.ds(b * 512, 512)
        widened = stream_ref[:, cols].astype(jnp.float32)
        normed_ref[:, cols] = (widened * inverse_rms * gain_ref[:, cols]).astype(jnp.bfloat16)


def combine(row_index, gates, returned, residual, gain):
    tokens, width = residual.shape
    part = returned.shape[2]
    vmem = pl.BlockSpec(memory_space=pltpu.VMEM)
    smem = pl.BlockSpec(memory_space=pltpu.SMEM)
    return pl.pallas_call(
        combine_kernel,
        in_specs=[smem, smem, vmem, vmem, vmem],
        out_specs=[vmem, vmem],
        out_shape=[jax.ShapeDtypeStruct((tokens, width), jnp.bfloat16)] * 2,
        scratch_shapes=[pltpu.VMEM((part // 128, tokens * column_parts, 128), jnp.float32)],
        compiler_params=pltpu.CompilerParams(vmem_limit_bytes=32 * MIB),
        cost_estimate=pl.CostEstimate(
            flops=20 * tokens * width, bytes_accessed=4 * MIB, transcendentals=0
        ),
    )(row_index, gates, returned, residual, gain)


def project_kernel(blocks, pieces, place_ref, shard_ref, *refs):
    normed_refs = refs[:blocks]
    piece_refs = refs[blocks : blocks + pieces]
    cos_ref, sin_ref, kept_ref, sent_ref, rows_scr, weight_scr, total, sems = refs[blocks + pieces :]
    copies = [
        pltpu.make_async_copy(piece_refs[p], weight_scr.at[p], sems.at[p]) for p in range(pieces)
    ]
    for copy in copies:
        copy.start()
    height = normed_refs[0].shape[0]
    for b in range(blocks):
        first = pl.multiple_of(place_ref[b], 32)
        rows_scr[pl.ds(first, height), :] = normed_refs[b][...]
    per_piece = piece_refs[0].shape[0] // 128
    for p in range(pieces):
        copies[p].wait()
        left = jnp.concatenate(
            [
                rows_scr[:, pl.ds(pl.multiple_of(shard_ref[p * per_piece + u] * 128, 128), 128)]
                for u in range(per_piece)
            ],
            axis=1,
        )
        part = jnp.dot(left, weight_scr[p], preferred_element_type=jnp.float32)
        if p == 0:
            total[...] = part
        else:
            total[...] += part
    heads = total.shape[1] // 128
    tokens = kept_ref.shape[0]
    for half, out_ref in ((0, kept_ref), (1, sent_ref)):
        rows = pl.ds(half * tokens, tokens)
        for h in range(heads):
            table = 1 if h == heads - 1 else 0
            cosine = cos_ref[table, rows, :]
            sine = sin_ref[table, rows, :]
            head = total[rows, h * 128 : (h + 1) * 128]
            turned = pltpu.roll(head, 64, 1)
            out_ref[:, h * 128 : (h + 1) * 128] = (head * cosine + turned * sine).astype(
                jnp.bfloat16
            )


def project(places, shards, normed_blocks, pieces, cosine, sine):
    blocks, count = len(normed_blocks), len(pieces)
    height, width = normed_blocks[0].shape
    depth, columns = pieces[0].shape
    rows = blocks * height
    vmem = pl.BlockSpec(memory_space=pltpu.VMEM)
    smem = pl.BlockSpec(memory_space=pltpu.SMEM)
    hbm = pl.BlockSpec(memory_space=pl.ANY)
    return pl.pallas_call(
        functools.partial(project_kernel, blocks, count),
        in_specs=[smem, smem] + [vmem] * blocks + [hbm] * count + [vmem] * 2,
        out_specs=[vmem, vmem],
        out_shape=[jax.ShapeDtypeStruct((rows // 2, columns), jnp.bfloat16)] * 2,
        scratch_shapes=[
            pltpu.VMEM((rows, width), jnp.bfloat16),
            pltpu.VMEM((count, depth, columns), jnp.bfloat16),
            pltpu.VMEM((rows, columns), jnp.float32),
            pltpu.SemaphoreType.DMA((count,)),
        ],
        compiler_params=pltpu.CompilerParams(vmem_limit_bytes=40 * MIB),
        cost_estimate=pl.CostEstimate(
            flops=2 * rows * width * columns, bytes_accessed=2 * width * columns, transcendentals=0
        ),
    )(places, shards, *normed_blocks, *pieces, cosine, sine)


query_chunk = 512
key_chunk = 1024


def split_queries(q_ref, turned, scale):
    for j in range(q_ref.shape[1] // 128):
        cols = pl.ds(j * 128, 128)
        scaled = q_ref[:, cols].astype(jnp.float32).T * scale
        high = scaled.astype(jnp.bfloat16)
        turned[:128, cols] = high
        turned[128:, cols] = (scaled - high.astype(jnp.float32)).astype(jnp.bfloat16)


def attend_block(turned, kv_ref, m_ref, l_ref, acc_ref, allowed):
    keys = kv_ref[:, :128]
    doubled = jnp.concatenate([keys, keys], axis=1)
    jobs = [
        (c, k)
        for k in range(kv_ref.shape[0] // key_chunk)
        for c in range(turned.shape[1] // query_chunk)
    ]

    def score(job):
        c, k = job
        return jnp.dot(
            doubled[k * key_chunk : (k + 1) * key_chunk],
            turned[:, pl.ds(c * query_chunk, query_chunk)],
            preferred_element_type=jnp.float32,
        )

    following = score(jobs[0])
    for n, (c, k) in enumerate(jobs):
        s = following
        if n + 1 < len(jobs):
            following = score(jobs[n + 1])
        cols = pl.ds(c * query_chunk, query_chunk)
        if allowed is not None:
            s = jnp.where(allowed(c, k), s, masked_score)
        m_old = m_ref[:, cols]
        m_new = jnp.maximum(m_old, jnp.max(s, axis=0, keepdims=True))
        factor = jnp.exp2(m_old - m_new)
        weights = jnp.exp2(s - m_new)
        m_ref[:, cols] = m_new
        l_ref[:, cols] = l_ref[:, cols] * factor + jnp.sum(weights, axis=0, keepdims=True)
        out = lax.dot_general(
            kv_ref[pl.ds(k * key_chunk, key_chunk), 128:],
            weights.astype(jnp.bfloat16),
            (((0,), (0,)), ((), ())),
            preferred_element_type=jnp.float32,
        )
        acc_ref[:, cols] = acc_ref[:, cols] * factor + out


def cache_kernel(scale, q_ref, kv_ref, m_ref, l_ref, acc_ref, turned):
    @pl.when(pl.program_id(0) == 0)
    def _():
        split_queries(q_ref, turned, scale)
        m_ref[...] = jnp.full_like(m_ref, masked_score)
        l_ref[...] = jnp.zeros_like(l_ref)
        acc_ref[...] = jnp.zeros_like(acc_ref)

    attend_block(turned, kv_ref, m_ref, l_ref, acc_ref, None)


def attend_cache(queries, cached, scale, block):
    tokens, width = queries.shape
    steps = cached.shape[0] // block
    whole = lambda i: (0, 0)
    return pl.pallas_call(
        functools.partial(cache_kernel, scale),
        grid=(steps,),
        in_specs=[
            pl.BlockSpec((tokens, width), whole),
            pl.BlockSpec((block, 256), lambda i: (i, 0)),
        ],
        out_specs=[
            pl.BlockSpec((1, tokens * width // 128), whole),
            pl.BlockSpec((1, tokens * width // 128), whole),
            pl.BlockSpec((128, tokens * width // 128), whole),
        ],
        out_shape=[
            jax.ShapeDtypeStruct((1, tokens * width // 128), jnp.float32),
            jax.ShapeDtypeStruct((1, tokens * width // 128), jnp.float32),
            jax.ShapeDtypeStruct((128, tokens * width // 128), jnp.float32),
        ],
        scratch_shapes=[pltpu.VMEM((256, tokens * width // 128), jnp.bfloat16)],
        compiler_params=pltpu.CompilerParams(vmem_limit_bytes=52 * MIB),
        cost_estimate=pl.CostEstimate(
            flops=8 * tokens * width * cached.shape[0],
            bytes_accessed=512 * cached.shape[0],
            transcendentals=tokens * width // 128 * cached.shape[0],
        ),
    )(queries, cached)


def span_kernel(
    scale, block, span_ref, q_ref, kv_ref, m_in, l_in, acc_in, o_ref, turned, m_ref, l_ref, acc_ref
):
    step = pl.program_id(0)
    tokens = q_ref.shape[0]
    first_query = span_ref[0] * tokens
    first_key = step * block

    @pl.when(step == 0)
    def _():
        split_queries(q_ref, turned, scale)
        m_ref[...] = m_in[...]
        l_ref[...] = l_in[...]
        acc_ref[...] = acc_in[...]

    @pl.when(first_key + block <= first_query)
    def _():
        attend_block(turned, kv_ref, m_ref, l_ref, acc_ref, None)

    def allowed(c, k):
        shape = (key_chunk, query_chunk)
        key = lax.broadcasted_iota(jnp.int32, shape, 0) + (first_key + k * key_chunk - first_query)
        token = lax.broadcasted_iota(jnp.int32, shape, 1) % tokens
        return key <= token

    @pl.when((first_key + block > first_query) & (first_key < first_query + tokens))
    def _():
        attend_block(turned, kv_ref, m_ref, l_ref, acc_ref, allowed)

    @pl.when(step == pl.num_programs(0) - 1)
    def _():
        for j in range(q_ref.shape[1] // 128):
            cols = pl.ds(j * 128, 128)
            o_ref[:, cols] = (acc_ref[:, cols] / l_ref[:, cols]).T.astype(jnp.bfloat16)


def attend_span(span, queries, keys_values, state, scale, block):
    tokens, width = queries.shape
    rows = tokens * width // 128
    steps = keys_values.shape[0] // block
    whole = lambda i, span_ref: (0, 0)
    needed = lambda i, span_ref: (
        jnp.minimum(i, (span_ref[0] * tokens + tokens - 1) // block),
        0,
    )
    return pl.pallas_call(
        functools.partial(span_kernel, scale, block),
        grid_spec=pltpu.PrefetchScalarGridSpec(
            num_scalar_prefetch=1,
            grid=(steps,),
            in_specs=[
                pl.BlockSpec((tokens, width), whole),
                pl.BlockSpec((block, 256), needed),
                pl.BlockSpec((1, rows), whole),
                pl.BlockSpec((1, rows), whole),
                pl.BlockSpec((128, rows), whole),
            ],
            out_specs=pl.BlockSpec((tokens, width), whole),
            scratch_shapes=[
                pltpu.VMEM((256, rows), jnp.bfloat16),
                pltpu.VMEM((1, rows), jnp.float32),
                pltpu.VMEM((1, rows), jnp.float32),
                pltpu.VMEM((128, rows), jnp.float32),
            ],
        ),
        out_shape=jax.ShapeDtypeStruct((tokens, width), jnp.bfloat16),
        compiler_params=pltpu.CompilerParams(vmem_limit_bytes=52 * MIB),
        cost_estimate=pl.CostEstimate(
            flops=8 * tokens * width * keys_values.shape[0],
            bytes_accessed=512 * keys_values.shape[0],
            transcendentals=rows * keys_values.shape[0],
        ),
    )(span, queries, keys_values, *state)


def shift(block, axis, by, size=4):
    return lax.ppermute(block, axis, [(i, (i + by) % size) for i in range(size)])


def ring_small(block, axis):
    return [shift(block, axis, 1), shift(block, axis, -1), shift(block, axis, 2)]


def ring_large(top, bottom, axis):
    before = [shift(top, axis, 1), shift(bottom, axis, 1)]
    after = [shift(top, axis, -1), shift(bottom, axis, -1)]
    opposite = [shift(before[0], axis, 1), shift(after[1], axis, -1)]
    return [top, bottom] + before + after + opposite


ring_steps = (0, -1, 1, 2)


def gather_weight(block, first_axis, second_axis):
    ring = [block] + ring_small(block, first_axis)
    top = jnp.concatenate(ring[:2], axis=0)
    bottom = jnp.concatenate(ring[2:], axis=0)
    return ring_large(top, bottom, second_axis)


def shard_order(first_is_x, x, zh, y):
    order = []
    for outer in ring_steps:
        for inner in ring_steps:
            dx, dy = (inner, outer) if first_is_x else (outer, inner)
            order.append(((x + dx) % 4) * 8 + zh * 4 + (y + dy) % 4)
    return order


def body(residual_in, expert_hidden, w_down, routes, gates, norm_gain, w_qkv, cache_kv):
    x, zh, y = lax.axis_index("x"), lax.axis_index("zh"), lax.axis_index("y")
    zl, core = lax.axis_index("zl"), lax.axis_index("c")
    seq_index = lax.axis_index(seq_axes)
    slot_cap = expert_hidden.shape[2]
    head_dim = cache_kv.shape[3]
    token_count, per_token = routes.shape
    seq_size = lax.axis_size(seq_axes)
    cache_length = cache_kv.shape[0] * seq_size
    tok_seq = token_count * lax.axis_size(head_axes)

    half_columns = w_qkv.shape[2] // 2
    weight_rows = w_qkv[:, 0, :]
    own_half = lax.dynamic_slice_in_dim(weight_rows, zh * half_columns, half_columns, axis=1)
    other_half = lax.dynamic_slice_in_dim(weight_rows, (1 - zh) * half_columns, half_columns, axis=1)
    partner_half = shift(other_half, "zh", 1, 2)
    pieces = gather_weight(own_half, "x", "y") + gather_weight(partner_half, "y", "x")
    shards = jnp.stack(shard_order(True, x, zh, y) + shard_order(False, x, 1 - zh, y))

    cached = lax.all_gather(cache_kv.reshape(-1, 2 * head_dim), seq_axes, axis=0, tiled=True)

    hidden = expert_hidden[0].reshape(-1, expert_hidden.shape[3])
    produced = expert_rows(hidden, w_down[0])
    returned = lax.all_to_all(produced, token_axes, split_axis=0, concat_axis=0, tiled=True)

    row_index = (routes * slot_cap + slot_numbers(routes)).reshape(-1)
    stream, normed = combine(
        row_index,
        gates.reshape(-1),
        returned.reshape(-1, column_parts, returned.shape[1]),
        residual_in,
        norm_gain[None, :],
    )

    z = zh * 2 + zl
    near = [normed] + [shift(normed, ("zh", "zl"), by) for by in (1, -1, 2)]
    far = [shift(block, "c", 1, 2) for block in near]
    places = []
    for c in (core, 1 - core):
        for by in ring_steps:
            source = (z + by) % 4
            other_span = ((source // 2) != zh).astype(jnp.int32)
            places.append(other_span * tok_seq + (source % 2) * 64 + c * 32)
    places = jnp.stack(places)

    half_dim = head_dim // 2
    inverse = rope_base ** (-2.0 * jnp.arange(half_dim, dtype=jnp.float32) / head_dim)
    partner_index = x * 8 + (1 - zh) * 4 + y
    steps = jnp.arange(tok_seq, dtype=jnp.int32)
    span_index = jnp.concatenate([seq_index * tok_seq + steps, partner_index * tok_seq + steps])
    angles = (span_index + cache_length).astype(jnp.float32)[:, None] * inverse[None, :]
    cosine = jnp.cos(angles)
    sine = jnp.sin(angles)
    cosine = jnp.concatenate([cosine, cosine], axis=1)
    sine = jnp.concatenate([-sine, sine], axis=1)
    plain = zh == 1
    cosine = jnp.stack([cosine, jnp.where(plain, 1.0, cosine)])
    sine = jnp.stack([sine, jnp.where(plain, 0.0, sine)])

    kept, sent = project(places, shards, near + far, pieces, cosine, sine)
    received = shift(sent, "zh", 1, 2)
    lower = jnp.where(zh == 0, kept, received)
    upper = jnp.where(zh == 0, received, kept)
    span_kv = upper[:, half_columns - 2 * head_dim :]
    queries = jnp.concatenate([lower, upper[:, : half_columns - 2 * head_dim]], axis=1)
    key_rows = lax.all_gather(span_kv, seq_axes, axis=0, tiled=True)

    scale = head_dim ** (-0.5) * log2_e
    state = attend_cache(queries, cached, scale, 2048)
    attended = attend_span(seq_index[None], queries, key_rows, state, scale, 1024)
    return (stream, attended[:, None, :])


def solution(mesh):
    fine = Mesh(mesh.devices.reshape(4, 2, 4, 2, 2), token_axes)
    in_specs = (
        P(token_axes, None),
        P(token_axes, None, None, None),
        P(token_axes, None, None),
        P(token_axes, None),
        P(token_axes, None),
        P(),
        P(seq_axes, head_axes, None),
        P(seq_axes, head_axes, None, None),
    )
    out_specs = (P(token_axes, None), P(seq_axes, head_axes, None))
    return jax.shard_map(body, mesh=fine, in_specs=in_specs, out_specs=out_specs, check_vma=False)
```

```python
import functools

import jax
import jax.numpy as jnp
from jax import lax
from jax.experimental import pallas as pl
from jax.experimental.pallas import tpu as pltpu
from jax.sharding import Mesh, PartitionSpec as P

rope_base = 1000000.0
masked_score = -1e30
log2_e = 1.4426950408889634

token_axes = ("x", "zh", "y", "zl", "c")
seq_axes = ("x", "zh", "y")
head_axes = ("zl", "c")

MIB = 2**20
column_parts = 8


def slot_numbers(route_block):
    flat_routes = route_block.reshape(-1)
    per_token = route_block.shape[1]
    token_of = jnp.arange(flat_routes.shape[0], dtype=jnp.int32) // per_token
    earlier = (flat_routes[:, None] == flat_routes[None, :]) & (
        token_of[None, :] < token_of[:, None]
    )
    return jnp.sum(earlier.astype(jnp.int32), axis=1).reshape(route_block.shape)


def expert_kernel(x_ref, w_ref, o_ref, scratch):
    step = pl.program_id(0)
    rows = x_ref.shape[0]
    product = jnp.dot(x_ref[...], w_ref[...], preferred_element_type=jnp.float32)
    for lane in range(product.shape[1] // 128):
        scratch[lane, pl.ds(step, rows, stride=column_parts), :] = product[
            :, lane * 128 : (lane + 1) * 128
        ]

    @pl.when(step == column_parts - 1)
    def _():
        for lane in range(product.shape[1] // 128):
            o_ref[:, lane * 128 : (lane + 1) * 128] = scratch[lane].astype(jnp.bfloat16)


def expert_rows(hidden, weight):
    rows, depth = hidden.shape
    width = weight.shape[1]
    part = width // column_parts
    return pl.pallas_call(
        expert_kernel,
        grid=(column_parts,),
        in_specs=[
            pl.BlockSpec((rows, depth), lambda b: (0, 0)),
            pl.BlockSpec((depth, part), lambda b: (0, b)),
        ],
        out_specs=pl.BlockSpec((rows * column_parts, part), lambda b: (0, 0)),
        out_shape=jax.ShapeDtypeStruct((rows * column_parts, part), jnp.bfloat16),
        scratch_shapes=[pltpu.VMEM((part // 128, rows * column_parts, 128), jnp.float32)],
        compiler_params=pltpu.CompilerParams(vmem_limit_bytes=58 * MIB),
        cost_estimate=pl.CostEstimate(
            flops=2 * rows * depth * width,
            bytes_accessed=2 * (depth * width + rows * (depth + width)),
            transcendentals=0,
        ),
    )(hidden, weight)


def combine_kernel(
    row_ref, gate_ref, got_ref, res_ref, gain_ref, stream_ref, planes_ref, normed_scr, scratch
):
    tokens, width = res_ref.shape
    per_token = row_ref.shape[0] // tokens
    part = got_ref.shape[2]

    def one(t, carry):
        total = jnp.zeros((column_parts, part), jnp.float32)
        for k in range(per_token):
            at = t * per_token + k
            total = total + gate_ref[at] * got_ref[row_ref[at]].astype(jnp.float32)
        first = pl.multiple_of(t * column_parts, column_parts)
        for lane in range(part // 128):
            scratch[lane, pl.ds(first, column_parts), :] = total[:, lane * 128 : (lane + 1) * 128]
        return carry

    lax.fori_loop(0, tokens, one, 0)
    squares = jnp.zeros((tokens, 128), jnp.float32)
    for b in range(column_parts):
        for lane in range(part // 128):
            cols = pl.ds(b * part + lane * 128, 128)
            moe = scratch[lane, pl.ds(b, tokens, stride=column_parts), :]
            stream = (res_ref[:, cols].astype(jnp.float32) + moe).astype(jnp.bfloat16)
            stream_ref[:, cols] = stream
            widened = stream.astype(jnp.float32)
            squares = squares + widened * widened
    mean = jnp.sum(squares, axis=1, keepdims=True) * (1.0 / width)
    inverse_rms = lax.rsqrt(mean + 1e-06)
    for b in range(width // 512):
        cols = pl.ds(b * 512, 512)
        widened = stream_ref[:, cols].astype(jnp.float32)
        normed_scr[:, cols] = (widened * inverse_rms * gain_ref[:, cols]).astype(jnp.bfloat16)
    for z in range(4):
        for u in range(width // 1024):
            first = u * 1024 + z // 2 * 512
            planes_ref[z * tokens : (z + 1) * tokens, u * 512 : (u + 1) * 512] = normed_scr[
                :, first : first + 512
            ]


def combine(row_index, gates, returned, residual, gain):
    tokens, width = residual.shape
    part = returned.shape[2]
    vmem = pl.BlockSpec(memory_space=pltpu.VMEM)
    smem = pl.BlockSpec(memory_space=pltpu.SMEM)
    return pl.pallas_call(
        combine_kernel,
        in_specs=[smem, smem, vmem, vmem, vmem],
        out_specs=[vmem] * 2,
        out_shape=[
            jax.ShapeDtypeStruct((tokens, width), jnp.bfloat16),
            jax.ShapeDtypeStruct((4 * tokens, width // 2), jnp.bfloat16),
        ],
        scratch_shapes=[
            pltpu.VMEM((tokens, width), jnp.bfloat16),
            pltpu.VMEM((part // 128, tokens * column_parts, 128), jnp.float32),
        ],
        compiler_params=pltpu.CompilerParams(vmem_limit_bytes=32 * MIB),
        cost_estimate=pl.CostEstimate(
            flops=20 * tokens * width, bytes_accessed=4 * MIB, transcendentals=0
        ),
    )(row_index, gates, returned, residual, gain)


weight_chunk = 512


def project_kernel(blocks, ranges, place_ref, *refs):
    normed_refs = refs[:blocks]
    weight_ref, kept_ref, sent_ref, rows_scr, weight_scr, total, sems = refs[blocks:]
    pieces = weight_ref.shape[0] // weight_chunk
    copies = []
    for p in range(pieces):
        rows, at = pl.ds(p * weight_chunk, weight_chunk), 0
        for n, (first, size) in enumerate(ranges):
            copies.append(
                pltpu.make_async_copy(
                    weight_ref.at[rows, pl.ds(first, size)],
                    weight_scr.at[rows, pl.ds(at, size)],
                    sems.at[p, n],
                )
            )
            at += size
    for copy in copies:
        copy.start()
    height = normed_refs[0].shape[0] // 4
    for b in range(4 * blocks):
        first = pl.multiple_of(place_ref[b], 32)
        rows_scr[pl.ds(first, height), :] = normed_refs[b // 4][
            b % 4 * height : (b % 4 + 1) * height, :
        ]
    for p in range(pieces):
        for n in range(len(ranges)):
            copies[p * len(ranges) + n].wait()
        rows = pl.ds(p * weight_chunk, weight_chunk)
        part = jnp.dot(rows_scr[:, rows], weight_scr[rows, :], preferred_element_type=jnp.float32)
        if p == 0:
            total[...] = part
        else:
            total[...] += part
    tokens = kept_ref.shape[0]
    kept_ref[...] = total[:tokens, :]
    sent_ref[...] = total[tokens:, :].astype(jnp.bfloat16)


def project(places, normed_blocks, weight, ranges):
    blocks = len(normed_blocks)
    height, depth = normed_blocks[0].shape
    columns = sum(size for _, size in ranges)
    rows = blocks * height
    vmem = pl.BlockSpec(memory_space=pltpu.VMEM)
    smem = pl.BlockSpec(memory_space=pltpu.SMEM)
    hbm = pl.BlockSpec(memory_space=pltpu.HBM)
    return pl.pallas_call(
        functools.partial(project_kernel, blocks, ranges),
        in_specs=[smem] + [vmem] * blocks + [hbm],
        out_specs=[vmem, vmem],
        out_shape=[
            jax.ShapeDtypeStruct((rows // 2, columns), jnp.float32),
            jax.ShapeDtypeStruct((rows // 2, columns), jnp.bfloat16),
        ],
        scratch_shapes=[
            pltpu.VMEM((rows, depth), jnp.bfloat16),
            pltpu.VMEM((depth, columns), jnp.bfloat16),
            pltpu.VMEM((rows, columns), jnp.float32),
            pltpu.SemaphoreType.DMA((depth // weight_chunk, len(ranges))),
        ],
        compiler_params=pltpu.CompilerParams(vmem_limit_bytes=58 * MIB),
        cost_estimate=pl.CostEstimate(
            flops=2 * rows * depth * columns, bytes_accessed=2 * depth * columns, transcendentals=0
        ),
    )(places, *normed_blocks, weight)


def rotated(kept_ref, received_ref, cos_ref, sin_ref, cols):
    head = kept_ref[:, cols] + received_ref[:, cols].astype(jnp.float32)
    turned = pltpu.roll(head, 64, 1)
    return (head * cos_ref[...] + turned * sin_ref[...]).astype(jnp.bfloat16)


def new_rows_kernel(kept_ref, received_ref, cos_ref, sin_ref, o_ref):
    first, tokens = kept_ref.shape[1] - 256, kept_ref.shape[0]
    keys = rotated(kept_ref, received_ref, cos_ref, sin_ref, pl.ds(first, 128))
    values = pl.ds(first + 128, 128)
    values = kept_ref[:, values] + received_ref[:, values].astype(jnp.float32)
    values = values.astype(jnp.bfloat16)
    for n in range(o_ref.shape[0] // tokens):
        o_ref[n * tokens : (n + 1) * tokens, :128] = keys
        o_ref[n * tokens : (n + 1) * tokens, 128:] = values


def new_rows(kept, received, cosine, sine, members):
    vmem = pl.BlockSpec(memory_space=pltpu.VMEM)
    return pl.pallas_call(
        new_rows_kernel,
        in_specs=[vmem] * 4,
        out_specs=vmem,
        out_shape=jax.ShapeDtypeStruct((members * kept.shape[0], 256), jnp.bfloat16),
        compiler_params=pltpu.CompilerParams(vmem_limit_bytes=58 * MIB),
    )(kept, received, cosine, sine)


query_chunk = 512
key_chunk = 1024


def split_queries(kept_ref, received_ref, cos_ref, sin_ref, turned, scale):
    for j in range(turned.shape[1] // 128):
        cols = slice(j * 128, (j + 1) * 128)
        head = rotated(kept_ref, received_ref, cos_ref, sin_ref, cols)
        scaled = head.astype(jnp.float32).T * scale
        high = scaled.astype(jnp.bfloat16)
        turned[:128, cols] = high
        turned[128:, cols] = (scaled - high.astype(jnp.float32)).astype(jnp.bfloat16)


def attend_rows(turned, take, chunks, m_ref, l_ref, acc_ref, allowed=None):
    jobs = [(c, k) for k in range(chunks) for c in range(turned.shape[1] // query_chunk)]

    def score(job):
        c, k = job
        keys = take(k, 0)
        return jnp.dot(
            jnp.concatenate([keys, keys], axis=1),
            turned[:, pl.ds(c * query_chunk, query_chunk)],
            preferred_element_type=jnp.float32,
        )

    following = score(jobs[0])
    for n, (c, k) in enumerate(jobs):
        s = following
        if n + 1 < len(jobs):
            following = score(jobs[n + 1])
        cols = pl.ds(c * query_chunk, query_chunk)
        if allowed is not None:
            s = jnp.where(allowed(c), s, masked_score)
        m_old = m_ref[:, cols]
        m_new = jnp.maximum(m_old, jnp.max(s, axis=0, keepdims=True))
        factor = jnp.exp2(m_old - m_new)
        weights = jnp.exp2(s - m_new)
        m_ref[:, cols] = m_new
        l_ref[:, cols] = l_ref[:, cols] * factor + jnp.sum(weights, axis=0, keepdims=True)
        out = lax.dot_general(
            take(k, 1),
            weights.astype(jnp.bfloat16),
            (((0,), (0,)), ((), ())),
            preferred_element_type=jnp.float32,
        )
        acc_ref[:, cols] = acc_ref[:, cols] * factor + out


def from_refs(refs):
    height = refs[0].shape[0]

    def take(k, which):
        cols = pl.ds(which * 128, 128)
        parts, first, last = [], k * key_chunk, (k + 1) * key_chunk
        for n, ref in enumerate(refs):
            low, high = max(first, n * height), min(last, (n + 1) * height)
            if low < high:
                parts.append(ref[pl.ds(low - n * height, high - low), cols])
        return parts[0] if len(parts) == 1 else jnp.concatenate(parts, axis=0)

    return take, len(refs) * height // key_chunk


def first_kernel(scale, count, kept_ref, received_ref, cos_ref, sin_ref, *refs):
    kv_refs = refs[:count]
    turned, m_ref, l_ref, acc_ref = refs[count:]
    split_queries(kept_ref, received_ref, cos_ref, sin_ref, turned, scale)
    m_ref[...] = jnp.full_like(m_ref, masked_score)
    l_ref[...] = jnp.zeros_like(l_ref)
    acc_ref[...] = jnp.zeros_like(acc_ref)
    take, chunks = from_refs(kv_refs)
    attend_rows(turned, take, chunks, m_ref, l_ref, acc_ref)


def next_kernel(count, turned, m_in, l_in, acc_in, *refs):
    kv_refs = refs[:count]
    m_ref, l_ref, acc_ref = refs[count:]
    m_ref[...] = m_in[...]
    l_ref[...] = l_in[...]
    acc_ref[...] = acc_in[...]
    take, chunks = from_refs(kv_refs)
    attend_rows(turned, take, chunks, m_ref, l_ref, acc_ref)


def attention_params(rows, keys):
    return dict(
        compiler_params=pltpu.CompilerParams(vmem_limit_bytes=58 * MIB),
        cost_estimate=pl.CostEstimate(
            flops=1024 * rows * keys, bytes_accessed=512 * keys, transcendentals=rows * keys
        ),
    )


def state_shapes(rows):
    return [
        jax.ShapeDtypeStruct((1, rows), jnp.float32),
        jax.ShapeDtypeStruct((1, rows), jnp.float32),
        jax.ShapeDtypeStruct((128, rows), jnp.float32),
    ]


def attend_first(heads, blocks, rows, scale):
    vmem = pl.BlockSpec(memory_space=pltpu.VMEM)
    return pl.pallas_call(
        functools.partial(first_kernel, scale, len(blocks)),
        in_specs=[vmem] * (len(heads) + len(blocks)),
        out_specs=[vmem] * 4,
        out_shape=[jax.ShapeDtypeStruct((256, rows), jnp.bfloat16)] + state_shapes(rows),
        **attention_params(rows, len(blocks) * blocks[0].shape[0]),
    )(*heads, *blocks)


def attend_next(state, blocks):
    turned, *rest = state
    rows = turned.shape[1]
    vmem = pl.BlockSpec(memory_space=pltpu.VMEM)
    rest = pl.pallas_call(
        functools.partial(next_kernel, len(blocks)),
        in_specs=[vmem] * (4 + len(blocks)),
        out_specs=[vmem] * 3,
        out_shape=state_shapes(rows),
        **attention_params(rows, len(blocks) * blocks[0].shape[0]),
    )(turned, *rest, *blocks)
    return [turned, *rest]


def span_kernel(tokens, span_ref, *refs):
    states = (refs[:4], refs[4:8])
    kv_ref, o_ref, m_ref, l_ref, acc_ref = refs[8:]
    rows = m_ref.shape[1]
    first_query = span_ref[0] * tokens
    last = first_query // key_chunk

    def taker(chunk):
        first = pl.multiple_of(chunk * key_chunk, key_chunk)
        return lambda k, which: kv_ref[pl.ds(first, key_chunk), which * 128 : (which + 1) * 128]

    def allowed(c):
        shape = (key_chunk, query_chunk)
        key = lax.broadcasted_iota(jnp.int32, shape, 0) + (last * key_chunk - first_query)
        token = lax.broadcasted_iota(jnp.int32, shape, 1) % tokens
        return key <= token

    for half, (turned, m_in, l_in, acc_in) in enumerate(states):
        m_ref[...] = m_in[...]
        l_ref[...] = l_in[...]
        acc_ref[...] = acc_in[...]

        def earlier(chunk, carry):
            attend_rows(turned, taker(chunk), 1, m_ref, l_ref, acc_ref)
            return carry

        lax.fori_loop(0, last, earlier, 0)
        attend_rows(turned, taker(last), 1, m_ref, l_ref, acc_ref, allowed)
        for j in range(rows // 128):
            cols = slice(j * 128, (j + 1) * 128)
            out = (acc_ref[:, cols] / l_ref[:, cols]).T.astype(jnp.bfloat16)
            o_ref[:, half * rows + j * 128 : half * rows + (j + 1) * 128] = out


def attend_span(span, first_state, second_state, key_rows, tokens):
    rows = first_state[0].shape[1]
    vmem = pl.BlockSpec(memory_space=pltpu.VMEM)
    smem = pl.BlockSpec(memory_space=pltpu.SMEM)
    return pl.pallas_call(
        functools.partial(span_kernel, tokens),
        in_specs=[smem] + [vmem] * 9,
        out_specs=vmem,
        out_shape=jax.ShapeDtypeStruct((tokens, 2 * rows * 128 // tokens), jnp.bfloat16),
        scratch_shapes=[
            pltpu.VMEM((1, rows), jnp.float32),
            pltpu.VMEM((1, rows), jnp.float32),
            pltpu.VMEM((128, rows), jnp.float32),
        ],
        **attention_params(2 * rows, key_rows.shape[0]),
    )(span, *first_state, *second_state, key_rows)


def shift(block, axis, by, size=4):
    return lax.ppermute(block, axis, [(i, (i + by) % size) for i in range(size)])


def ring(block, axis):
    return [shift(block, axis, by) for by in (1, -1, 2)]


def body(residual_in, expert_hidden, w_down, routes, gates, norm_gain, w_qkv, cache_kv):
    x, zh, y = lax.axis_index("x"), lax.axis_index("zh"), lax.axis_index("y")
    zl, core = lax.axis_index("zl"), lax.axis_index("c")
    seq_index = lax.axis_index(seq_axes)
    slot_cap = expert_hidden.shape[2]
    head_dim = cache_kv.shape[3]
    token_count, per_token = routes.shape
    seq_size = lax.axis_size(seq_axes)
    cache_length = cache_kv.shape[0] * seq_size
    tok_seq = token_count * lax.axis_size(head_axes)

    weight = lax.all_gather(w_qkv[:, 0, :], ("x", "y"), axis=0, tiled=True)

    own_cache = cache_kv.reshape(-1, 2 * head_dim)
    partner_cache = shift(own_cache, "zh", 1, 2)
    hidden = expert_hidden[0].reshape(-1, expert_hidden.shape[3])
    produced = expert_rows(hidden, w_down[0])
    returned = lax.all_to_all(produced, token_axes, split_axis=0, concat_axis=0, tiled=True)
    first_ring = [own_cache] + ring(own_cache, "x")
    second_ring = [partner_cache] + ring(partner_cache, "y")

    row_index = (routes * slot_cap + slot_numbers(routes)).reshape(-1)
    stream, planes = combine(
        row_index,
        gates.reshape(-1),
        returned.reshape(-1, column_parts, returned.shape[1]),
        residual_in,
        norm_gain[None, :],
    )
    near = lax.all_to_all(planes, ("zh", "zl"), split_axis=0, concat_axis=0, tiled=True)
    near, first_ring, second_ring = lax.optimization_barrier((near, first_ring, second_ring))
    far = shift(near, "c", 1, 2)
    first_cache = jnp.concatenate(first_ring, axis=0)
    second_cache = jnp.concatenate(second_ring, axis=0)
    first_others = ring(first_cache, "y")
    second_others = ring(second_cache, "x")
    places = jnp.stack(
        [
            jnp.where(zh == z // 2, 0, tok_seq) + z % 2 * 2 * token_count + c * token_count
            for c in (core, 1 - core)
            for z in range(4)
        ]
    )

    half_dim = head_dim // 2
    inverse = rope_base ** (-2.0 * jnp.arange(half_dim, dtype=jnp.float32) / head_dim)
    span_index = seq_index * tok_seq + jnp.arange(tok_seq, dtype=jnp.int32)
    angles = (span_index + cache_length).astype(jnp.float32)[:, None] * inverse[None, :]
    cosine = jnp.cos(angles)
    sine = jnp.sin(angles)
    cosine = jnp.concatenate([cosine, cosine], axis=1)
    sine = jnp.concatenate([-sine, sine], axis=1)

    half = (w_qkv.shape[2] - 2 * head_dim) // 2
    first_kept, first_sent = project(
        places, [near, far], weight, ((0, half), (2 * half, 2 * head_dim))
    )
    first_received = shift(first_sent, "zh", 1, 2)
    second_kept, second_sent = project(places, [near, far], weight, ((half, half),))
    second_received = shift(second_sent, "zh", 1, 2)
    span_kv = new_rows(first_kept, first_received, cosine, sine, seq_size)
    key_rows = lax.all_to_all(span_kv, seq_axes, split_axis=0, concat_axis=0, tiled=True)

    scale = head_dim ** (-0.5) * log2_e
    rows = tok_seq * half // head_dim
    first_heads = (first_kept, first_received, cosine, sine)
    second_heads = (second_kept, second_received, cosine, sine)
    first_part = [first_cache, second_cache] + first_others[:2]
    second_part = second_others + first_others[2:]
    first_state = attend_first(first_heads, first_part, rows, scale)
    second_state = attend_first(second_heads, first_part, rows, scale)
    first_state = attend_next(first_state, second_part)
    second_state = attend_next(second_state, second_part)
    attended = attend_span(seq_index[None], first_state, second_state, key_rows, tok_seq)
    return (stream, attended[:, None, :])


def solution(mesh):
    fine = Mesh(mesh.devices.reshape(4, 2, 4, 2, 2), token_axes)
    in_specs = (
        P(token_axes, None),
        P(token_axes, None, None, None),
        P(token_axes, None, None),
        P(token_axes, None),
        P(token_axes, None),
        P(),
        P(seq_axes, head_axes, None),
        P(seq_axes, head_axes, None, None),
    )
    out_specs = (P(token_axes, None), P(seq_axes, head_axes, None))
    return jax.shard_map(body, mesh=fine, in_specs=in_specs, out_specs=out_specs, check_vma=False)
```

```python
import functools

import jax
import jax.numpy as jnp
from jax import lax
from jax.experimental import pallas as pl
from jax.experimental.pallas import tpu as pltpu
from jax.sharding import Mesh, PartitionSpec as P

rope_base = 1000000.0
masked_score = -1e30
log2_e = 1.4426950408889634

token_axes = ("x", "zh", "y", "zl", "c")
seq_axes = ("x", "zh", "y")
head_axes = ("zl", "c")

MIB = 2**20
column_parts = 8


def slot_numbers(route_block):
    flat_routes = route_block.reshape(-1)
    per_token = route_block.shape[1]
    token_of = jnp.arange(flat_routes.shape[0], dtype=jnp.int32) // per_token
    earlier = (flat_routes[:, None] == flat_routes[None, :]) & (
        token_of[None, :] < token_of[:, None]
    )
    return jnp.sum(earlier.astype(jnp.int32), axis=1).reshape(route_block.shape)


def expert_kernel(x_ref, w_ref, o_ref, scratch):
    step = pl.program_id(0)
    rows = x_ref.shape[0]
    product = jnp.dot(x_ref[...], w_ref[...], preferred_element_type=jnp.float32)
    for lane in range(product.shape[1] // 128):
        scratch[lane, pl.ds(step, rows, stride=column_parts), :] = product[
            :, lane * 128 : (lane + 1) * 128
        ]

    @pl.when(step == column_parts - 1)
    def _():
        for lane in range(product.shape[1] // 128):
            o_ref[:, lane * 128 : (lane + 1) * 128] = scratch[lane].astype(jnp.bfloat16)


def expert_rows(hidden, weight):
    rows, depth = hidden.shape
    width = weight.shape[1]
    part = width // column_parts
    return pl.pallas_call(
        expert_kernel,
        grid=(column_parts,),
        in_specs=[
            pl.BlockSpec((rows, depth), lambda b: (0, 0)),
            pl.BlockSpec((depth, part), lambda b: (0, b)),
        ],
        out_specs=pl.BlockSpec((rows * column_parts, part), lambda b: (0, 0)),
        out_shape=jax.ShapeDtypeStruct((rows * column_parts, part), jnp.bfloat16),
        scratch_shapes=[pltpu.VMEM((part // 128, rows * column_parts, 128), jnp.float32)],
        compiler_params=pltpu.CompilerParams(vmem_limit_bytes=58 * MIB),
        cost_estimate=pl.CostEstimate(
            flops=2 * rows * depth * width,
            bytes_accessed=2 * (depth * width + rows * (depth + width)),
            transcendentals=0,
        ),
    )(hidden, weight)


def combine_kernel(
    row_ref, gate_ref, got_ref, res_ref, gain_ref, stream_ref, planes_ref, normed_scr, scratch
):
    tokens, width = res_ref.shape
    per_token = row_ref.shape[0] // tokens
    part = got_ref.shape[2]

    def one(t, carry):
        total = jnp.zeros((column_parts, part), jnp.float32)
        for k in range(per_token):
            at = t * per_token + k
            total = total + gate_ref[at] * got_ref[row_ref[at]].astype(jnp.float32)
        first = pl.multiple_of(t * column_parts, column_parts)
        for lane in range(part // 128):
            scratch[lane, pl.ds(first, column_parts), :] = total[:, lane * 128 : (lane + 1) * 128]
        return carry

    lax.fori_loop(0, tokens, one, 0)
    squares = jnp.zeros((tokens, 128), jnp.float32)
    for b in range(column_parts):
        for lane in range(part // 128):
            cols = pl.ds(b * part + lane * 128, 128)
            moe = scratch[lane, pl.ds(b, tokens, stride=column_parts), :]
            stream = (res_ref[:, cols].astype(jnp.float32) + moe).astype(jnp.bfloat16)
            stream_ref[:, cols] = stream
            widened = stream.astype(jnp.float32)
            squares = squares + widened * widened
    mean = jnp.sum(squares, axis=1, keepdims=True) * (1.0 / width)
    inverse_rms = lax.rsqrt(mean + 1e-06)
    for b in range(width // 512):
        cols = pl.ds(b * 512, 512)
        widened = stream_ref[:, cols].astype(jnp.float32)
        normed_scr[:, cols] = (widened * inverse_rms * gain_ref[:, cols]).astype(jnp.bfloat16)
    for z in range(4):
        for u in range(width // 1024):
            first = u * 1024 + z // 2 * 512
            planes_ref[z * tokens : (z + 1) * tokens, u * 512 : (u + 1) * 512] = normed_scr[
                :, first : first + 512
            ]


def combine(row_index, gates, returned, residual, gain):
    tokens, width = residual.shape
    part = returned.shape[2]
    vmem = pl.BlockSpec(memory_space=pltpu.VMEM)
    smem = pl.BlockSpec(memory_space=pltpu.SMEM)
    return pl.pallas_call(
        combine_kernel,
        in_specs=[smem, smem, vmem, vmem, vmem],
        out_specs=[vmem] * 2,
        out_shape=[
            jax.ShapeDtypeStruct((tokens, width), jnp.bfloat16),
            jax.ShapeDtypeStruct((4 * tokens, width // 2), jnp.bfloat16),
        ],
        scratch_shapes=[
            pltpu.VMEM((tokens, width), jnp.bfloat16),
            pltpu.VMEM((part // 128, tokens * column_parts, 128), jnp.float32),
        ],
        compiler_params=pltpu.CompilerParams(vmem_limit_bytes=32 * MIB),
        cost_estimate=pl.CostEstimate(
            flops=20 * tokens * width, bytes_accessed=4 * MIB, transcendentals=0
        ),
    )(row_index, gates, returned, residual, gain)


weight_chunk = 512


def project_kernel(blocks, ranges, place_ref, *refs):
    normed_refs = refs[:blocks]
    weight_ref, kept_ref, sent_ref, rows_scr, weight_scr, total, sems = refs[blocks:]
    pieces = weight_ref.shape[0] // weight_chunk
    copies = []
    for p in range(pieces):
        rows, at = pl.ds(p * weight_chunk, weight_chunk), 0
        for n, (first, size) in enumerate(ranges):
            copies.append(
                pltpu.make_async_copy(
                    weight_ref.at[rows, pl.ds(first, size)],
                    weight_scr.at[rows, pl.ds(at, size)],
                    sems.at[p, n],
                )
            )
            at += size
    for copy in copies:
        copy.start()
    height = normed_refs[0].shape[0] // 4
    for b in range(4 * blocks):
        first = pl.multiple_of(place_ref[b], 32)
        rows_scr[pl.ds(first, height), :] = normed_refs[b // 4][
            b % 4 * height : (b % 4 + 1) * height, :
        ]
    for p in range(pieces):
        for n in range(len(ranges)):
            copies[p * len(ranges) + n].wait()
        rows = pl.ds(p * weight_chunk, weight_chunk)
        part = jnp.dot(rows_scr[:, rows], weight_scr[rows, :], preferred_element_type=jnp.float32)
        if p == 0:
            total[...] = part
        else:
            total[...] += part
    tokens = kept_ref.shape[0]
    kept_ref[...] = total[:tokens, :]
    sent_ref[...] = total[tokens:, :].astype(jnp.bfloat16)


def project(places, normed_blocks, weight, ranges):
    blocks = len(normed_blocks)
    height, depth = normed_blocks[0].shape
    columns = sum(size for _, size in ranges)
    rows = blocks * height
    vmem = pl.BlockSpec(memory_space=pltpu.VMEM)
    smem = pl.BlockSpec(memory_space=pltpu.SMEM)
    hbm = pl.BlockSpec(memory_space=pltpu.HBM)
    return pl.pallas_call(
        functools.partial(project_kernel, blocks, ranges),
        in_specs=[smem] + [vmem] * blocks + [hbm],
        out_specs=[vmem, vmem],
        out_shape=[
            jax.ShapeDtypeStruct((rows // 2, columns), jnp.float32),
            jax.ShapeDtypeStruct((rows // 2, columns), jnp.bfloat16),
        ],
        scratch_shapes=[
            pltpu.VMEM((rows, depth), jnp.bfloat16),
            pltpu.VMEM((depth, columns), jnp.bfloat16),
            pltpu.VMEM((rows, columns), jnp.float32),
            pltpu.SemaphoreType.DMA((depth // weight_chunk, len(ranges))),
        ],
        compiler_params=pltpu.CompilerParams(vmem_limit_bytes=58 * MIB),
        cost_estimate=pl.CostEstimate(
            flops=2 * rows * depth * columns, bytes_accessed=2 * depth * columns, transcendentals=0
        ),
    )(places, *normed_blocks, weight)


def rotated(kept_ref, received_ref, cos_ref, sin_ref, cols):
    head = kept_ref[:, cols] + received_ref[:, cols].astype(jnp.float32)
    turned = pltpu.roll(head, 64, 1)
    return (head * cos_ref[...] + turned * sin_ref[...]).astype(jnp.bfloat16)


def new_rows_kernel(kept_ref, received_ref, cos_ref, sin_ref, o_ref):
    first, tokens = kept_ref.shape[1] - 256, kept_ref.shape[0]
    keys = rotated(kept_ref, received_ref, cos_ref, sin_ref, pl.ds(first, 128))
    values = pl.ds(first + 128, 128)
    values = kept_ref[:, values] + received_ref[:, values].astype(jnp.float32)
    values = values.astype(jnp.bfloat16)
    for n in range(o_ref.shape[0] // tokens):
        o_ref[n * tokens : (n + 1) * tokens, :128] = keys
        o_ref[n * tokens : (n + 1) * tokens, 128:] = values


def new_rows(kept, received, cosine, sine, members):
    vmem = pl.BlockSpec(memory_space=pltpu.VMEM)
    return pl.pallas_call(
        new_rows_kernel,
        in_specs=[vmem] * 4,
        out_specs=vmem,
        out_shape=jax.ShapeDtypeStruct((members * kept.shape[0], 256), jnp.bfloat16),
        compiler_params=pltpu.CompilerParams(vmem_limit_bytes=58 * MIB),
    )(kept, received, cosine, sine)


query_chunk = 512
key_chunk = 1024


def split_queries(kept_ref, received_ref, cos_ref, sin_ref, turned, scale):
    for j in range(turned.shape[1] // 128):
        cols = slice(j * 128, (j + 1) * 128)
        head = rotated(kept_ref, received_ref, cos_ref, sin_ref, cols)
        scaled = head.astype(jnp.float32).T * scale
        high = scaled.astype(jnp.bfloat16)
        turned[:128, cols] = high
        turned[128:, cols] = (scaled - high.astype(jnp.float32)).astype(jnp.bfloat16)


def attend_rows(turned, take, chunks, m_ref, l_ref, acc_ref, allowed=None):
    jobs = [(c, k) for k in range(chunks) for c in range(turned.shape[1] // query_chunk)]

    def score(job):
        c, k = job
        keys = take(k, 0)
        return jnp.dot(
            jnp.concatenate([keys, keys], axis=1),
            turned[:, pl.ds(c * query_chunk, query_chunk)],
            preferred_element_type=jnp.float32,
        )

    following = score(jobs[0])
    for n, (c, k) in enumerate(jobs):
        s = following
        if n + 1 < len(jobs):
            following = score(jobs[n + 1])
        cols = pl.ds(c * query_chunk, query_chunk)
        if allowed is not None:
            s = jnp.where(allowed(c), s, masked_score)
        m_old = m_ref[:, cols]
        m_new = jnp.maximum(m_old, jnp.max(s, axis=0, keepdims=True))
        factor = jnp.exp2(m_old - m_new)
        weights = jnp.exp2(s - m_new)
        m_ref[:, cols] = m_new
        l_ref[:, cols] = l_ref[:, cols] * factor + jnp.sum(weights, axis=0, keepdims=True)
        out = lax.dot_general(
            take(k, 1),
            weights.astype(jnp.bfloat16),
            (((0,), (0,)), ((), ())),
            preferred_element_type=jnp.float32,
        )
        acc_ref[:, cols] = acc_ref[:, cols] * factor + out


def from_refs(refs):
    height = refs[0].shape[0]

    def take(k, which):
        cols = pl.ds(which * 128, 128)
        parts, first, last = [], k * key_chunk, (k + 1) * key_chunk
        for n, ref in enumerate(refs):
            low, high = max(first, n * height), min(last, (n + 1) * height)
            if low < high:
                parts.append(ref[pl.ds(low - n * height, high - low), cols])
        return parts[0] if len(parts) == 1 else jnp.concatenate(parts, axis=0)

    return take, len(refs) * height // key_chunk


def first_kernel(scale, count, kept_ref, received_ref, cos_ref, sin_ref, *refs):
    kv_refs = refs[:count]
    turned, m_ref, l_ref, acc_ref = refs[count:]
    split_queries(kept_ref, received_ref, cos_ref, sin_ref, turned, scale)
    m_ref[...] = jnp.full_like(m_ref, masked_score)
    l_ref[...] = jnp.zeros_like(l_ref)
    acc_ref[...] = jnp.zeros_like(acc_ref)
    take, chunks = from_refs(kv_refs)
    attend_rows(turned, take, chunks, m_ref, l_ref, acc_ref)


def next_kernel(count, turned, m_in, l_in, acc_in, *refs):
    kv_refs = refs[:count]
    m_ref, l_ref, acc_ref = refs[count:]
    m_ref[...] = m_in[...]
    l_ref[...] = l_in[...]
    acc_ref[...] = acc_in[...]
    take, chunks = from_refs(kv_refs)
    attend_rows(turned, take, chunks, m_ref, l_ref, acc_ref)


def attention_params(rows, keys, limit=36):
    return dict(
        compiler_params=pltpu.CompilerParams(vmem_limit_bytes=limit * MIB),
        cost_estimate=pl.CostEstimate(
            flops=1024 * rows * keys, bytes_accessed=512 * keys, transcendentals=rows * keys
        ),
    )


def state_shapes(rows):
    return [
        jax.ShapeDtypeStruct((1, rows), jnp.float32),
        jax.ShapeDtypeStruct((1, rows), jnp.float32),
        jax.ShapeDtypeStruct((128, rows), jnp.float32),
    ]


def attend_first(heads, blocks, rows, scale, limit):
    vmem = pl.BlockSpec(memory_space=pltpu.VMEM)
    return pl.pallas_call(
        functools.partial(first_kernel, scale, len(blocks)),
        in_specs=[vmem] * (len(heads) + len(blocks)),
        out_specs=[vmem] * 4,
        out_shape=[jax.ShapeDtypeStruct((256, rows), jnp.bfloat16)] + state_shapes(rows),
        **attention_params(rows, len(blocks) * blocks[0].shape[0], limit),
    )(*heads, *blocks)


def attend_next(state, blocks):
    turned, *rest = state
    rows = turned.shape[1]
    vmem = pl.BlockSpec(memory_space=pltpu.VMEM)
    rest = pl.pallas_call(
        functools.partial(next_kernel, len(blocks)),
        in_specs=[vmem] * (4 + len(blocks)),
        out_specs=[vmem] * 3,
        out_shape=state_shapes(rows),
        **attention_params(rows, len(blocks) * blocks[0].shape[0]),
    )(turned, *rest, *blocks)
    return [turned, *rest]


def span_kernel(tokens, span_ref, *refs):
    states = (refs[:4], refs[4:8])
    kv_ref, o_ref, turned, m_ref, l_ref, acc_ref = refs[8:]
    rows = refs[1].shape[1]
    for half, state in enumerate(states):
        cols = slice(half * rows, (half + 1) * rows)
        for to_ref, from_ref in zip((turned, m_ref, l_ref, acc_ref), state):
            to_ref[:, cols] = from_ref[...]
    first_query = span_ref[0] * tokens
    last = first_query // key_chunk

    def taker(chunk):
        def take(k, which):
            first = pl.multiple_of((chunk + k) * key_chunk, key_chunk)
            return kv_ref[pl.ds(first, key_chunk), which * 128 : (which + 1) * 128]

        return take

    @pl.when(last >= 2)
    def _():
        attend_rows(turned, taker(0), 2, m_ref, l_ref, acc_ref)

    @pl.when(last % 2 == 1)
    def _():
        attend_rows(turned, taker(last - 1), 1, m_ref, l_ref, acc_ref)

    key = lax.broadcasted_iota(jnp.int32, (key_chunk, 1), 0) + (last * key_chunk - first_query)

    def allowed(c):
        token = lax.broadcasted_iota(jnp.int32, (1, query_chunk), 1) % tokens
        return key <= token

    attend_rows(turned, taker(last), 1, m_ref, l_ref, acc_ref, allowed)
    inverse = 1.0 / l_ref[...]
    for j in range(acc_ref.shape[1] // 128):
        cols = slice(j * 128, (j + 1) * 128)
        o_ref[:, cols] = (acc_ref[:, cols] * inverse[:, cols]).T.astype(jnp.bfloat16)


def attend_span(span, first_state, second_state, key_rows, tokens):
    rows = first_state[0].shape[1]
    vmem = pl.BlockSpec(memory_space=pltpu.VMEM)
    smem = pl.BlockSpec(memory_space=pltpu.SMEM)
    return pl.pallas_call(
        functools.partial(span_kernel, tokens),
        in_specs=[smem] + [vmem] * 9,
        out_specs=vmem,
        out_shape=jax.ShapeDtypeStruct((tokens, 2 * rows * 128 // tokens), jnp.bfloat16),
        scratch_shapes=[
            pltpu.VMEM((256, 2 * rows), jnp.bfloat16),
            pltpu.VMEM((1, 2 * rows), jnp.float32),
            pltpu.VMEM((1, 2 * rows), jnp.float32),
            pltpu.VMEM((128, 2 * rows), jnp.float32),
        ],
        **attention_params(2 * rows, key_rows.shape[0], 58),
    )(span, *first_state, *second_state, key_rows)


def shift(block, axis, by, size=4):
    return lax.ppermute(block, axis, [(i, (i + by) % size) for i in range(size)])


def ring(block, axis):
    return [shift(block, axis, by) for by in (1, -1, 2)]


def body(residual_in, expert_hidden, w_down, routes, gates, norm_gain, w_qkv, cache_kv):
    x, zh, y = lax.axis_index("x"), lax.axis_index("zh"), lax.axis_index("y")
    zl, core = lax.axis_index("zl"), lax.axis_index("c")
    seq_index = lax.axis_index(seq_axes)
    slot_cap = expert_hidden.shape[2]
    head_dim = cache_kv.shape[3]
    token_count, per_token = routes.shape
    seq_size = lax.axis_size(seq_axes)
    cache_length = cache_kv.shape[0] * seq_size
    tok_seq = token_count * lax.axis_size(head_axes)

    weight = lax.all_gather(w_qkv[:, 0, :], ("x", "y"), axis=0, tiled=True)

    own_cache = cache_kv.reshape(-1, 2 * head_dim)
    partner_cache = shift(own_cache, "zh", 1, 2)
    hidden = expert_hidden[0].reshape(-1, expert_hidden.shape[3])
    produced = expert_rows(hidden, w_down[0])
    returned = lax.all_to_all(produced, token_axes, split_axis=0, concat_axis=0, tiled=True)
    first_ring = [own_cache] + ring(own_cache, "x")
    second_ring = [partner_cache] + ring(partner_cache, "y")

    row_index = (routes * slot_cap + slot_numbers(routes)).reshape(-1)
    stream, planes = combine(
        row_index,
        gates.reshape(-1),
        returned.reshape(-1, column_parts, returned.shape[1]),
        residual_in,
        norm_gain[None, :],
    )
    near = lax.all_to_all(planes, ("zh", "zl"), split_axis=0, concat_axis=0, tiled=True)
    near, first_ring, second_ring = lax.optimization_barrier((near, first_ring, second_ring))
    far = shift(near, "c", 1, 2)
    first_cache = jnp.concatenate(first_ring, axis=0)
    second_cache = jnp.concatenate(second_ring, axis=0)
    first_others = ring(first_cache, "y")
    second_others = ring(second_cache, "x")
    places = jnp.stack(
        [
            jnp.where(zh == z // 2, 0, tok_seq) + z % 2 * 2 * token_count + c * token_count
            for c in (core, 1 - core)
            for z in range(4)
        ]
    )

    half_dim = head_dim // 2
    inverse = rope_base ** (-2.0 * jnp.arange(half_dim, dtype=jnp.float32) / head_dim)
    span_index = seq_index * tok_seq + jnp.arange(tok_seq, dtype=jnp.int32)
    angles = (span_index + cache_length).astype(jnp.float32)[:, None] * inverse[None, :]
    cosine = jnp.cos(angles)
    sine = jnp.sin(angles)
    cosine = jnp.concatenate([cosine, cosine], axis=1)
    sine = jnp.concatenate([-sine, sine], axis=1)

    half = (w_qkv.shape[2] - 2 * head_dim) // 2
    first_kept, first_sent = project(
        places, [near, far], weight, ((0, half), (2 * half, 2 * head_dim))
    )
    first_received = shift(first_sent, "zh", 1, 2)
    second_kept, second_sent = project(places, [near, far], weight, ((half, half),))
    second_received = shift(second_sent, "zh", 1, 2)
    span_kv = new_rows(first_kept, first_received, cosine, sine, seq_size)
    key_rows = lax.all_to_all(span_kv, seq_axes, split_axis=0, concat_axis=0, tiled=True)

    scale = head_dim ** (-0.5) * log2_e
    rows = tok_seq * half // head_dim
    first_heads = (first_kept, first_received, cosine, sine)
    second_heads = (second_kept, second_received, cosine, sine)
    first_part = [first_cache, second_cache] + first_others[:2]
    second_part = second_others + first_others[2:]
    first_state = attend_first(first_heads, first_part, rows, scale, 58)
    second_state = attend_first(second_heads, first_part, rows, scale, 36)
    first_state = attend_next(first_state, second_part)
    second_state = attend_next(second_state, second_part)
    attended = attend_span(seq_index[None], first_state, second_state, key_rows, tok_seq)
    return (stream, attended[:, None, :])


def solution(mesh):
    fine = Mesh(mesh.devices.reshape(4, 2, 4, 2, 2), token_axes)
    in_specs = (
        P(token_axes, None),
        P(token_axes, None, None, None),
        P(token_axes, None, None),
        P(token_axes, None),
        P(token_axes, None),
        P(),
        P(seq_axes, head_axes, None),
        P(seq_axes, head_axes, None, None),
    )
    out_specs = (P(token_axes, None), P(seq_axes, head_axes, None))
    return jax.shard_map(body, mesh=fine, in_specs=in_specs, out_specs=out_specs, check_vma=False)
```

```python
import functools

import jax
import jax.numpy as jnp
from jax import lax
from jax.experimental import pallas as pl
from jax.experimental.pallas import tpu as pltpu
from jax.sharding import Mesh, PartitionSpec as P

rope_base = 1000000.0
masked_score = -1e30
log2_e = 1.4426950408889634

token_axes = ("x", "zh", "y", "zl", "c")
seq_axes = ("x", "zh", "y")
head_axes = ("zl", "c")

MIB = 2**20
column_parts = 8


def slot_numbers(route_block):
    flat_routes = route_block.reshape(-1)
    per_token = route_block.shape[1]
    token_of = jnp.arange(flat_routes.shape[0], dtype=jnp.int32) // per_token
    earlier = (flat_routes[:, None] == flat_routes[None, :]) & (
        token_of[None, :] < token_of[:, None]
    )
    return jnp.sum(earlier.astype(jnp.int32), axis=1).reshape(route_block.shape)


def expert_kernel(x_ref, w_ref, o_ref, scratch):
    step = pl.program_id(0)
    rows = x_ref.shape[0]
    product = jnp.dot(x_ref[...], w_ref[...], preferred_element_type=jnp.float32)
    for lane in range(product.shape[1] // 128):
        scratch[lane, pl.ds(step, rows, stride=column_parts), :] = product[
            :, lane * 128 : (lane + 1) * 128
        ]

    @pl.when(step == column_parts - 1)
    def _():
        for lane in range(product.shape[1] // 128):
            o_ref[:, lane * 128 : (lane + 1) * 128] = scratch[lane].astype(jnp.bfloat16)


def expert_rows(hidden, weight):
    rows, depth = hidden.shape
    width = weight.shape[1]
    part = width // column_parts
    return pl.pallas_call(
        expert_kernel,
        grid=(column_parts,),
        in_specs=[
            pl.BlockSpec((rows, depth), lambda b: (0, 0)),
            pl.BlockSpec((depth, part), lambda b: (0, b)),
        ],
        out_specs=pl.BlockSpec((rows * column_parts, part), lambda b: (0, 0)),
        out_shape=jax.ShapeDtypeStruct((rows * column_parts, part), jnp.bfloat16),
        scratch_shapes=[pltpu.VMEM((part // 128, rows * column_parts, 128), jnp.float32)],
        compiler_params=pltpu.CompilerParams(vmem_limit_bytes=58 * MIB),
        cost_estimate=pl.CostEstimate(
            flops=2 * rows * depth * width,
            bytes_accessed=2 * (depth * width + rows * (depth + width)),
            transcendentals=0,
        ),
    )(hidden, weight)


def combine_kernel(
    row_ref, gate_ref, got_ref, res_ref, gain_ref, stream_ref, planes_ref, normed_scr, scratch
):
    tokens, width = res_ref.shape
    per_token = row_ref.shape[0] // tokens
    part = got_ref.shape[2]

    def one(t, carry):
        total = jnp.zeros((column_parts, part), jnp.float32)
        for k in range(per_token):
            at = t * per_token + k
            total = total + gate_ref[at] * got_ref[row_ref[at]].astype(jnp.float32)
        first = pl.multiple_of(t * column_parts, column_parts)
        for lane in range(part // 128):
            scratch[lane, pl.ds(first, column_parts), :] = total[:, lane * 128 : (lane + 1) * 128]
        return carry

    lax.fori_loop(0, tokens, one, 0)
    squares = jnp.zeros((tokens, 128), jnp.float32)
    for b in range(column_parts):
        for lane in range(part // 128):
            cols = pl.ds(b * part + lane * 128, 128)
            moe = scratch[lane, pl.ds(b, tokens, stride=column_parts), :]
            stream = (res_ref[:, cols].astype(jnp.float32) + moe).astype(jnp.bfloat16)
            stream_ref[:, cols] = stream
            widened = stream.astype(jnp.float32)
            squares = squares + widened * widened
    mean = jnp.sum(squares, axis=1, keepdims=True) * (1.0 / width)
    inverse_rms = lax.rsqrt(mean + 1e-06)
    for b in range(width // 512):
        cols = pl.ds(b * 512, 512)
        widened = stream_ref[:, cols].astype(jnp.float32)
        normed_scr[:, cols] = (widened * inverse_rms * gain_ref[:, cols]).astype(jnp.bfloat16)
    for z in range(4):
        for u in range(width // 1024):
            first = u * 1024 + z // 2 * 512
            planes_ref[z * tokens : (z + 1) * tokens, u * 512 : (u + 1) * 512] = normed_scr[
                :, first : first + 512
            ]


def combine(row_index, gates, returned, residual, gain):
    tokens, width = residual.shape
    part = returned.shape[2]
    vmem = pl.BlockSpec(memory_space=pltpu.VMEM)
    smem = pl.BlockSpec(memory_space=pltpu.SMEM)
    return pl.pallas_call(
        combine_kernel,
        in_specs=[smem, smem, vmem, vmem, vmem],
        out_specs=[vmem] * 2,
        out_shape=[
            jax.ShapeDtypeStruct((tokens, width), jnp.bfloat16),
            jax.ShapeDtypeStruct((4 * tokens, width // 2), jnp.bfloat16),
        ],
        scratch_shapes=[
            pltpu.VMEM((tokens, width), jnp.bfloat16),
            pltpu.VMEM((part // 128, tokens * column_parts, 128), jnp.float32),
        ],
        compiler_params=pltpu.CompilerParams(vmem_limit_bytes=32 * MIB),
        cost_estimate=pl.CostEstimate(
            flops=20 * tokens * width, bytes_accessed=4 * MIB, transcendentals=0
        ),
    )(row_index, gates, returned, residual, gain)


weight_chunk = 512


def project_kernel(blocks, ranges, place_ref, *refs):
    normed_refs = refs[:blocks]
    weight_ref, kept_ref, sent_ref, rows_scr, weight_scr, total, sems = refs[blocks:]
    pieces = weight_ref.shape[0] // weight_chunk
    copies = []
    for p in range(pieces):
        rows, at = pl.ds(p * weight_chunk, weight_chunk), 0
        for n, (first, size) in enumerate(ranges):
            copies.append(
                pltpu.make_async_copy(
                    weight_ref.at[rows, pl.ds(first, size)],
                    weight_scr.at[rows, pl.ds(at, size)],
                    sems.at[p, n],
                )
            )
            at += size
    for copy in copies:
        copy.start()
    height = normed_refs[0].shape[0] // 4
    for b in range(4 * blocks):
        first = pl.multiple_of(place_ref[b], 32)
        rows_scr[pl.ds(first, height), :] = normed_refs[b // 4][
            b % 4 * height : (b % 4 + 1) * height, :
        ]
    for p in range(pieces):
        for n in range(len(ranges)):
            copies[p * len(ranges) + n].wait()
        rows = pl.ds(p * weight_chunk, weight_chunk)
        part = jnp.dot(rows_scr[:, rows], weight_scr[rows, :], preferred_element_type=jnp.float32)
        if p == 0:
            total[...] = part
        else:
            total[...] += part
    tokens = kept_ref.shape[0]
    kept_ref[...] = total[:tokens, :]
    sent_ref[...] = total[tokens:, :].astype(jnp.bfloat16)


def project(places, normed_blocks, weight, ranges):
    blocks = len(normed_blocks)
    height, depth = normed_blocks[0].shape
    columns = sum(size for _, size in ranges)
    rows = blocks * height
    vmem = pl.BlockSpec(memory_space=pltpu.VMEM)
    smem = pl.BlockSpec(memory_space=pltpu.SMEM)
    hbm = pl.BlockSpec(memory_space=pltpu.HBM)
    return pl.pallas_call(
        functools.partial(project_kernel, blocks, ranges),
        in_specs=[smem] + [vmem] * blocks + [hbm],
        out_specs=[vmem, vmem],
        out_shape=[
            jax.ShapeDtypeStruct((rows // 2, columns), jnp.float32),
            jax.ShapeDtypeStruct((rows // 2, columns), jnp.bfloat16),
        ],
        scratch_shapes=[
            pltpu.VMEM((rows, depth), jnp.bfloat16),
            pltpu.VMEM((depth, columns), jnp.bfloat16),
            pltpu.VMEM((rows, columns), jnp.float32),
            pltpu.SemaphoreType.DMA((depth // weight_chunk, len(ranges))),
        ],
        compiler_params=pltpu.CompilerParams(vmem_limit_bytes=58 * MIB),
        cost_estimate=pl.CostEstimate(
            flops=2 * rows * depth * columns, bytes_accessed=2 * depth * columns, transcendentals=0
        ),
    )(places, *normed_blocks, weight)


def rotated(kept_ref, received_ref, cos_ref, sin_ref, cols):
    head = kept_ref[:, cols] + received_ref[:, cols].astype(jnp.float32)
    turned = pltpu.roll(head, 64, 1)
    return (head * cos_ref[...] + turned * sin_ref[...]).astype(jnp.bfloat16)


def new_rows_kernel(kept_ref, received_ref, cos_ref, sin_ref, o_ref):
    first, tokens = kept_ref.shape[1] - 256, kept_ref.shape[0]
    keys = rotated(kept_ref, received_ref, cos_ref, sin_ref, pl.ds(first, 128))
    values = pl.ds(first + 128, 128)
    values = kept_ref[:, values] + received_ref[:, values].astype(jnp.float32)
    values = values.astype(jnp.bfloat16)
    for n in range(o_ref.shape[0] // tokens):
        o_ref[n * tokens : (n + 1) * tokens, :128] = keys
        o_ref[n * tokens : (n + 1) * tokens, 128:] = values


def new_rows(kept, received, cosine, sine, members):
    vmem = pl.BlockSpec(memory_space=pltpu.VMEM)
    return pl.pallas_call(
        new_rows_kernel,
        in_specs=[vmem] * 4,
        out_specs=vmem,
        out_shape=jax.ShapeDtypeStruct((members * kept.shape[0], 256), jnp.bfloat16),
        compiler_params=pltpu.CompilerParams(vmem_limit_bytes=58 * MIB),
    )(kept, received, cosine, sine)


query_chunk = 512
key_chunk = 1024


def split_queries(kept_ref, received_ref, cos_ref, sin_ref, turned, scale):
    for j in range(turned.shape[1] // 128):
        cols = slice(j * 128, (j + 1) * 128)
        head = rotated(kept_ref, received_ref, cos_ref, sin_ref, cols)
        scaled = head.astype(jnp.float32).T * scale
        high = scaled.astype(jnp.bfloat16)
        turned[:128, cols] = high
        turned[128:, cols] = (scaled - high.astype(jnp.float32)).astype(jnp.bfloat16)


def attend_rows(turned, take, chunks, m_ref, l_ref, acc_ref, allowed=None):
    jobs = [(c, k) for k in range(chunks) for c in range(turned.shape[1] // query_chunk)]

    def score(job):
        c, k = job
        keys = take(k, 0)
        return jnp.dot(
            jnp.concatenate([keys, keys], axis=1),
            turned[:, pl.ds(c * query_chunk, query_chunk)],
            preferred_element_type=jnp.float32,
        )

    following = score(jobs[0])
    for n, (c, k) in enumerate(jobs):
        s = following
        if n + 1 < len(jobs):
            following = score(jobs[n + 1])
        cols = pl.ds(c * query_chunk, query_chunk)
        if allowed is not None:
            s = jnp.where(allowed(c), s, masked_score)
        m_old = m_ref[:, cols]
        m_new = jnp.maximum(m_old, jnp.max(s, axis=0, keepdims=True))
        factor = jnp.exp2(m_old - m_new)
        weights = jnp.exp2(s - m_new)
        m_ref[:, cols] = m_new
        l_ref[:, cols] = l_ref[:, cols] * factor + jnp.sum(weights, axis=0, keepdims=True)
        out = lax.dot_general(
            take(k, 1),
            weights.astype(jnp.bfloat16),
            (((0,), (0,)), ((), ())),
            preferred_element_type=jnp.float32,
        )
        acc_ref[:, cols] = acc_ref[:, cols] * factor + out


def from_refs(refs):
    height = refs[0].shape[0]

    def take(k, which):
        cols = pl.ds(which * 128, 128)
        parts, first, last = [], k * key_chunk, (k + 1) * key_chunk
        for n, ref in enumerate(refs):
            low, high = max(first, n * height), min(last, (n + 1) * height)
            if low < high:
                parts.append(ref[pl.ds(low - n * height, high - low), cols])
        return parts[0] if len(parts) == 1 else jnp.concatenate(parts, axis=0)

    return take, len(refs) * height // key_chunk


def first_kernel(scale, count, kept_ref, received_ref, cos_ref, sin_ref, *refs):
    kv_refs = refs[:count]
    turned, m_ref, l_ref, acc_ref = refs[count:]
    split_queries(kept_ref, received_ref, cos_ref, sin_ref, turned, scale)
    m_ref[...] = jnp.full_like(m_ref, masked_score)
    l_ref[...] = jnp.zeros_like(l_ref)
    acc_ref[...] = jnp.zeros_like(acc_ref)
    take, chunks = from_refs(kv_refs)
    attend_rows(turned, take, chunks, m_ref, l_ref, acc_ref)


def next_kernel(count, turned, m_in, l_in, acc_in, *refs):
    kv_refs = refs[:count]
    m_ref, l_ref, acc_ref = refs[count:]
    m_ref[...] = m_in[...]
    l_ref[...] = l_in[...]
    acc_ref[...] = acc_in[...]
    take, chunks = from_refs(kv_refs)
    attend_rows(turned, take, chunks, m_ref, l_ref, acc_ref)


def attention_params(rows, keys):
    return dict(
        compiler_params=pltpu.CompilerParams(vmem_limit_bytes=36 * MIB),
        cost_estimate=pl.CostEstimate(
            flops=1024 * rows * keys, bytes_accessed=512 * keys, transcendentals=rows * keys
        ),
    )


def state_shapes(rows):
    return [
        jax.ShapeDtypeStruct((1, rows), jnp.float32),
        jax.ShapeDtypeStruct((1, rows), jnp.float32),
        jax.ShapeDtypeStruct((128, rows), jnp.float32),
    ]


def attend_first(heads, blocks, rows, scale):
    vmem = pl.BlockSpec(memory_space=pltpu.VMEM)
    return pl.pallas_call(
        functools.partial(first_kernel, scale, len(blocks)),
        in_specs=[vmem] * (len(heads) + len(blocks)),
        out_specs=[vmem] * 4,
        out_shape=[jax.ShapeDtypeStruct((256, rows), jnp.bfloat16)] + state_shapes(rows),
        **attention_params(rows, len(blocks) * blocks[0].shape[0]),
    )(*heads, *blocks)


def attend_next(state, blocks):
    turned, *rest = state
    rows = turned.shape[1]
    vmem = pl.BlockSpec(memory_space=pltpu.VMEM)
    rest = pl.pallas_call(
        functools.partial(next_kernel, len(blocks)),
        in_specs=[vmem] * (4 + len(blocks)),
        out_specs=[vmem] * 3,
        out_shape=state_shapes(rows),
        **attention_params(rows, len(blocks) * blocks[0].shape[0]),
    )(turned, *rest, *blocks)
    return [turned, *rest]


def span_kernel(tokens, span_ref, *refs):
    states = (refs[:4], refs[4:8])
    kv_ref, o_ref, turned, m_ref, l_ref, acc_ref = refs[8:]
    rows = refs[1].shape[1]
    for half, state in enumerate(states):
        cols = slice(half * rows, (half + 1) * rows)
        for to_ref, from_ref in zip((turned, m_ref, l_ref, acc_ref), state):
            to_ref[:, cols] = from_ref[...]
    first_query = span_ref[0] * tokens
    last = first_query // key_chunk

    def taker(chunk):
        def take(k, which):
            first = pl.multiple_of((chunk + k) * key_chunk, key_chunk)
            return kv_ref[pl.ds(first, key_chunk), which * 128 : (which + 1) * 128]

        return take

    @pl.when(last >= 2)
    def _():
        attend_rows(turned, taker(0), 2, m_ref, l_ref, acc_ref)

    @pl.when(last % 2 == 1)
    def _():
        attend_rows(turned, taker(last - 1), 1, m_ref, l_ref, acc_ref)

    key = lax.broadcasted_iota(jnp.int32, (key_chunk, 1), 0) + (last * key_chunk - first_query)

    def allowed(c):
        token = lax.broadcasted_iota(jnp.int32, (1, query_chunk), 1) % tokens
        return key <= token

    attend_rows(turned, taker(last), 1, m_ref, l_ref, acc_ref, allowed)
    inverse = 1.0 / l_ref[...]
    for j in range(acc_ref.shape[1] // 128):
        cols = slice(j * 128, (j + 1) * 128)
        o_ref[:, cols] = (acc_ref[:, cols] * inverse[:, cols]).T.astype(jnp.bfloat16)


def attend_span(span, first_state, second_state, key_rows, tokens):
    rows = first_state[0].shape[1]
    vmem = pl.BlockSpec(memory_space=pltpu.VMEM)
    smem = pl.BlockSpec(memory_space=pltpu.SMEM)
    return pl.pallas_call(
        functools.partial(span_kernel, tokens),
        in_specs=[smem] + [vmem] * 9,
        out_specs=vmem,
        out_shape=jax.ShapeDtypeStruct((tokens, 2 * rows * 128 // tokens), jnp.bfloat16),
        scratch_shapes=[
            pltpu.VMEM((256, 2 * rows), jnp.bfloat16),
            pltpu.VMEM((1, 2 * rows), jnp.float32),
            pltpu.VMEM((1, 2 * rows), jnp.float32),
            pltpu.VMEM((128, 2 * rows), jnp.float32),
        ],
        **attention_params(2 * rows, key_rows.shape[0]),
    )(span, *first_state, *second_state, key_rows)


def shift(block, axis, by, size=4):
    return lax.ppermute(block, axis, [(i, (i + by) % size) for i in range(size)])


def ring(block, axis):
    return [shift(block, axis, by) for by in (1, -1, 2)]


def body(residual_in, expert_hidden, w_down, routes, gates, norm_gain, w_qkv, cache_kv):
    x, zh, y = lax.axis_index("x"), lax.axis_index("zh"), lax.axis_index("y")
    zl, core = lax.axis_index("zl"), lax.axis_index("c")
    seq_index = lax.axis_index(seq_axes)
    slot_cap = expert_hidden.shape[2]
    head_dim = cache_kv.shape[3]
    token_count, per_token = routes.shape
    seq_size = lax.axis_size(seq_axes)
    cache_length = cache_kv.shape[0] * seq_size
    tok_seq = token_count * lax.axis_size(head_axes)

    weight = lax.all_gather(w_qkv[:, 0, :], ("x", "y"), axis=0, tiled=True)

    own_cache = cache_kv.reshape(-1, 2 * head_dim)
    partner_cache = shift(own_cache, "zh", 1, 2)
    hidden = expert_hidden[0].reshape(-1, expert_hidden.shape[3])
    produced = expert_rows(hidden, w_down[0])
    returned = lax.all_to_all(produced, token_axes, split_axis=0, concat_axis=0, tiled=True)
    first_ring = [own_cache] + ring(own_cache, "x")
    second_ring = [partner_cache] + ring(partner_cache, "y")

    row_index = (routes * slot_cap + slot_numbers(routes)).reshape(-1)
    stream, planes = combine(
        row_index,
        gates.reshape(-1),
        returned.reshape(-1, column_parts, returned.shape[1]),
        residual_in,
        norm_gain[None, :],
    )
    near = lax.all_to_all(planes, ("zh", "zl"), split_axis=0, concat_axis=0, tiled=True)
    near, first_ring, second_ring = lax.optimization_barrier((near, first_ring, second_ring))
    far = shift(near, "c", 1, 2)
    first_cache = jnp.concatenate(first_ring, axis=0)
    second_cache = jnp.concatenate(second_ring, axis=0)
    first_others = ring(first_cache, "y")
    second_others = ring(second_cache, "x")
    places = jnp.stack(
        [
            jnp.where(zh == z // 2, 0, tok_seq) + z % 2 * 2 * token_count + c * token_count
            for c in (core, 1 - core)
            for z in range(4)
        ]
    )

    half_dim = head_dim // 2
    inverse = rope_base ** (-2.0 * jnp.arange(half_dim, dtype=jnp.float32) / head_dim)
    span_index = seq_index * tok_seq + jnp.arange(tok_seq, dtype=jnp.int32)
    angles = (span_index + cache_length).astype(jnp.float32)[:, None] * inverse[None, :]
    cosine = jnp.cos(angles)
    sine = jnp.sin(angles)
    cosine = jnp.concatenate([cosine, cosine], axis=1)
    sine = jnp.concatenate([-sine, sine], axis=1)

    half = (w_qkv.shape[2] - 2 * head_dim) // 2
    first_kept, first_sent = project(
        places, [near, far], weight, ((0, half), (2 * half, 2 * head_dim))
    )
    first_received = shift(first_sent, "zh", 1, 2)
    second_kept, second_sent = project(places, [near, far], weight, ((half, half),))
    second_received = shift(second_sent, "zh", 1, 2)
    span_kv = new_rows(first_kept, first_received, cosine, sine, seq_size)
    key_rows = lax.all_to_all(span_kv, seq_axes, split_axis=0, concat_axis=0, tiled=True)

    scale = head_dim ** (-0.5) * log2_e
    rows = tok_seq * half // head_dim
    first_heads = (first_kept, first_received, cosine, sine)
    second_heads = (second_kept, second_received, cosine, sine)
    first_part = [first_cache, second_cache] + first_others[:2]
    second_part = second_others + first_others[2:]
    first_state = attend_first(first_heads, first_part, rows, scale)
    second_state = attend_first(second_heads, first_part, rows, scale)
    first_state = attend_next(first_state, second_part)
    second_state = attend_next(second_state, second_part)
    attended = attend_span(seq_index[None], first_state, second_state, key_rows, tok_seq)
    return (stream, attended[:, None, :])


def solution(mesh):
    fine = Mesh(mesh.devices.reshape(4, 2, 4, 2, 2), token_axes)
    in_specs = (
        P(token_axes, None),
        P(token_axes, None, None, None),
        P(token_axes, None, None),
        P(token_axes, None),
        P(token_axes, None),
        P(),
        P(seq_axes, head_axes, None),
        P(seq_axes, head_axes, None, None),
    )
    out_specs = (P(token_axes, None), P(seq_axes, head_axes, None))
    return jax.shard_map(body, mesh=fine, in_specs=in_specs, out_specs=out_specs, check_vma=False)
```

```python
import functools

import jax
import jax.numpy as jnp
from jax import lax
from jax.experimental import pallas as pl
from jax.experimental.pallas import tpu as pltpu
from jax.sharding import Mesh, PartitionSpec as P

rope_base = 1000000.0
masked_score = -1e30
log2_e = 1.4426950408889634

token_axes = ("x", "zh", "y", "zl", "c")
seq_axes = ("x", "zh", "y")
head_axes = ("zl", "c")

MIB = 2**20
column_parts = 8


def slot_numbers(route_block):
    flat_routes = route_block.reshape(-1)
    per_token = route_block.shape[1]
    token_of = jnp.arange(flat_routes.shape[0], dtype=jnp.int32) // per_token
    earlier = (flat_routes[:, None] == flat_routes[None, :]) & (
        token_of[None, :] < token_of[:, None]
    )
    return jnp.sum(earlier.astype(jnp.int32), axis=1).reshape(route_block.shape)


def expert_kernel(x_ref, w_ref, o_ref, scratch):
    step = pl.program_id(0)
    rows = x_ref.shape[0]
    product = jnp.dot(x_ref[...], w_ref[...], preferred_element_type=jnp.float32)
    for lane in range(product.shape[1] // 128):
        scratch[lane, pl.ds(step, rows, stride=column_parts), :] = product[
            :, lane * 128 : (lane + 1) * 128
        ]

    @pl.when(step == column_parts - 1)
    def _():
        for lane in range(product.shape[1] // 128):
            o_ref[:, lane * 128 : (lane + 1) * 128] = scratch[lane].astype(jnp.bfloat16)


def expert_rows(hidden, weight):
    rows, depth = hidden.shape
    width = weight.shape[1]
    part = width // column_parts
    return pl.pallas_call(
        expert_kernel,
        grid=(column_parts,),
        in_specs=[
            pl.BlockSpec((rows, depth), lambda b: (0, 0)),
            pl.BlockSpec((depth, part), lambda b: (0, b)),
        ],
        out_specs=pl.BlockSpec((rows * column_parts, part), lambda b: (0, 0)),
        out_shape=jax.ShapeDtypeStruct((rows * column_parts, part), jnp.bfloat16),
        scratch_shapes=[pltpu.VMEM((part // 128, rows * column_parts, 128), jnp.float32)],
        compiler_params=pltpu.CompilerParams(vmem_limit_bytes=58 * MIB),
        cost_estimate=pl.CostEstimate(
            flops=2 * rows * depth * width,
            bytes_accessed=2 * (depth * width + rows * (depth + width)),
            transcendentals=0,
        ),
    )(hidden, weight)


def combine_kernel(
    row_ref, gate_ref, got_ref, res_ref, gain_ref, stream_ref, planes_ref, normed_scr, scratch
):
    tokens, width = res_ref.shape
    per_token = row_ref.shape[0] // tokens
    part = got_ref.shape[2]

    def one(t, carry):
        total = jnp.zeros((column_parts, part), jnp.float32)
        for k in range(per_token):
            at = t * per_token + k
            total = total + gate_ref[at] * got_ref[row_ref[at]].astype(jnp.float32)
        first = pl.multiple_of(t * column_parts, column_parts)
        for lane in range(part // 128):
            scratch[lane, pl.ds(first, column_parts), :] = total[:, lane * 128 : (lane + 1) * 128]
        return carry

    lax.fori_loop(0, tokens, one, 0)
    squares = jnp.zeros((tokens, 128), jnp.float32)
    for b in range(column_parts):
        for lane in range(part // 128):
            cols = pl.ds(b * part + lane * 128, 128)
            moe = scratch[lane, pl.ds(b, tokens, stride=column_parts), :]
            stream = (res_ref[:, cols].astype(jnp.float32) + moe).astype(jnp.bfloat16)
            stream_ref[:, cols] = stream
            widened = stream.astype(jnp.float32)
            squares = squares + widened * widened
    mean = jnp.sum(squares, axis=1, keepdims=True) * (1.0 / width)
    inverse_rms = lax.rsqrt(mean + 1e-06)
    for b in range(width // 512):
        cols = pl.ds(b * 512, 512)
        widened = stream_ref[:, cols].astype(jnp.float32)
        normed_scr[:, cols] = (widened * inverse_rms * gain_ref[:, cols]).astype(jnp.bfloat16)
    for z in range(4):
        for u in range(width // 1024):
            first = u * 1024 + z // 2 * 512
            planes_ref[z * tokens : (z + 1) * tokens, u * 512 : (u + 1) * 512] = normed_scr[
                :, first : first + 512
            ]


def combine(row_index, gates, returned, residual, gain):
    tokens, width = residual.shape
    part = returned.shape[2]
    vmem = pl.BlockSpec(memory_space=pltpu.VMEM)
    smem = pl.BlockSpec(memory_space=pltpu.SMEM)
    return pl.pallas_call(
        combine_kernel,
        in_specs=[smem, smem, vmem, vmem, vmem],
        out_specs=[vmem] * 2,
        out_shape=[
            jax.ShapeDtypeStruct((tokens, width), jnp.bfloat16),
            jax.ShapeDtypeStruct((4 * tokens, width // 2), jnp.bfloat16),
        ],
        scratch_shapes=[
            pltpu.VMEM((tokens, width), jnp.bfloat16),
            pltpu.VMEM((part // 128, tokens * column_parts, 128), jnp.float32),
        ],
        compiler_params=pltpu.CompilerParams(vmem_limit_bytes=32 * MIB),
        cost_estimate=pl.CostEstimate(
            flops=20 * tokens * width, bytes_accessed=4 * MIB, transcendentals=0
        ),
    )(row_index, gates, returned, residual, gain)


weight_chunk = 512


def project_kernel(blocks, ranges, place_ref, *refs):
    normed_refs = refs[:blocks]
    weight_ref, kept_ref, sent_ref, rows_scr, weight_scr, total, sems = refs[blocks:]
    pieces = weight_ref.shape[0] // weight_chunk
    copies = []
    for p in range(pieces):
        rows, at = pl.ds(p * weight_chunk, weight_chunk), 0
        for n, (first, size) in enumerate(ranges):
            copies.append(
                pltpu.make_async_copy(
                    weight_ref.at[rows, pl.ds(first, size)],
                    weight_scr.at[rows, pl.ds(at, size)],
                    sems.at[p, n],
                )
            )
            at += size
    for copy in copies:
        copy.start()
    height = normed_refs[0].shape[0] // 4
    for b in range(4 * blocks):
        first = pl.multiple_of(place_ref[b], 32)
        rows_scr[pl.ds(first, height), :] = normed_refs[b // 4][
            b % 4 * height : (b % 4 + 1) * height, :
        ]
    for p in range(pieces):
        for n in range(len(ranges)):
            copies[p * len(ranges) + n].wait()
        rows = pl.ds(p * weight_chunk, weight_chunk)
        part = jnp.dot(rows_scr[:, rows], weight_scr[rows, :], preferred_element_type=jnp.float32)
        if p == 0:
            total[...] = part
        else:
            total[...] += part
    tokens = kept_ref.shape[0]
    kept_ref[...] = total[:tokens, :]
    sent_ref[...] = total[tokens:, :].astype(jnp.bfloat16)


def project(places, normed_blocks, weight, ranges):
    blocks = len(normed_blocks)
    height, depth = normed_blocks[0].shape
    columns = sum(size for _, size in ranges)
    rows = blocks * height
    vmem = pl.BlockSpec(memory_space=pltpu.VMEM)
    smem = pl.BlockSpec(memory_space=pltpu.SMEM)
    hbm = pl.BlockSpec(memory_space=pltpu.HBM)
    return pl.pallas_call(
        functools.partial(project_kernel, blocks, ranges),
        in_specs=[smem] + [vmem] * blocks + [hbm],
        out_specs=[vmem, vmem],
        out_shape=[
            jax.ShapeDtypeStruct((rows // 2, columns), jnp.float32),
            jax.ShapeDtypeStruct((rows // 2, columns), jnp.bfloat16),
        ],
        scratch_shapes=[
            pltpu.VMEM((rows, depth), jnp.bfloat16),
            pltpu.VMEM((depth, columns), jnp.bfloat16),
            pltpu.VMEM((rows, columns), jnp.float32),
            pltpu.SemaphoreType.DMA((depth // weight_chunk, len(ranges))),
        ],
        compiler_params=pltpu.CompilerParams(vmem_limit_bytes=58 * MIB),
        cost_estimate=pl.CostEstimate(
            flops=2 * rows * depth * columns, bytes_accessed=2 * depth * columns, transcendentals=0
        ),
    )(places, *normed_blocks, weight)


def rotated(kept_ref, received_ref, cos_ref, sin_ref, cols):
    head = kept_ref[:, cols] + received_ref[:, cols].astype(jnp.float32)
    turned = pltpu.roll(head, 64, 1)
    return (head * cos_ref[...] + turned * sin_ref[...]).astype(jnp.bfloat16)


def new_rows_kernel(kept_ref, received_ref, cos_ref, sin_ref, o_ref):
    first, tokens = kept_ref.shape[1] - 256, kept_ref.shape[0]
    keys = rotated(kept_ref, received_ref, cos_ref, sin_ref, pl.ds(first, 128))
    values = pl.ds(first + 128, 128)
    values = kept_ref[:, values] + received_ref[:, values].astype(jnp.float32)
    values = values.astype(jnp.bfloat16)
    for n in range(o_ref.shape[0] // tokens):
        o_ref[n * tokens : (n + 1) * tokens, :128] = keys
        o_ref[n * tokens : (n + 1) * tokens, 128:] = values


def new_rows(kept, received, cosine, sine, members):
    vmem = pl.BlockSpec(memory_space=pltpu.VMEM)
    return pl.pallas_call(
        new_rows_kernel,
        in_specs=[vmem] * 4,
        out_specs=vmem,
        out_shape=jax.ShapeDtypeStruct((members * kept.shape[0], 256), jnp.bfloat16),
        compiler_params=pltpu.CompilerParams(vmem_limit_bytes=20 * MIB),
    )(kept, received, cosine, sine)


query_chunk = 512
key_chunk = 1024


def split_queries(kept_ref, received_ref, cos_ref, sin_ref, turned, scale):
    for j in range(turned.shape[1] // 128):
        cols = slice(j * 128, (j + 1) * 128)
        head = rotated(kept_ref, received_ref, cos_ref, sin_ref, cols)
        scaled = head.astype(jnp.float32).T * scale
        high = scaled.astype(jnp.bfloat16)
        turned[:128, cols] = high
        turned[128:, cols] = (scaled - high.astype(jnp.float32)).astype(jnp.bfloat16)


def attend_rows(turned, take, chunks, m_ref, l_ref, acc_ref, allowed=None):
    jobs = [(c, k) for k in range(chunks) for c in range(turned.shape[1] // query_chunk)]

    def score(job):
        c, k = job
        keys = take(k, 0)
        return jnp.dot(
            jnp.concatenate([keys, keys], axis=1),
            turned[:, pl.ds(c * query_chunk, query_chunk)],
            preferred_element_type=jnp.float32,
        )

    following = score(jobs[0])
    for n, (c, k) in enumerate(jobs):
        s = following
        if n + 1 < len(jobs):
            following = score(jobs[n + 1])
        cols = pl.ds(c * query_chunk, query_chunk)
        if allowed is not None:
            s = jnp.where(allowed(c), s, masked_score)
        m_old = m_ref[:, cols]
        m_new = jnp.maximum(m_old, jnp.max(s, axis=0, keepdims=True))
        factor = jnp.exp2(m_old - m_new)
        weights = jnp.exp2(s - m_new)
        m_ref[:, cols] = m_new
        l_ref[:, cols] = l_ref[:, cols] * factor + jnp.sum(weights, axis=0, keepdims=True)
        out = lax.dot_general(
            take(k, 1),
            weights.astype(jnp.bfloat16),
            (((0,), (0,)), ((), ())),
            preferred_element_type=jnp.float32,
        )
        acc_ref[:, cols] = acc_ref[:, cols] * factor + out


def from_refs(refs):
    height = refs[0].shape[0]

    def take(k, which):
        cols = pl.ds(which * 128, 128)
        parts, first, last = [], k * key_chunk, (k + 1) * key_chunk
        for n, ref in enumerate(refs):
            low, high = max(first, n * height), min(last, (n + 1) * height)
            if low < high:
                parts.append(ref[pl.ds(low - n * height, high - low), cols])
        return parts[0] if len(parts) == 1 else jnp.concatenate(parts, axis=0)

    return take, len(refs) * height // key_chunk


def first_kernel(scale, count, kept_ref, received_ref, cos_ref, sin_ref, *refs):
    kv_refs = refs[:count]
    turned, m_ref, l_ref, acc_ref = refs[count:]
    split_queries(kept_ref, received_ref, cos_ref, sin_ref, turned, scale)
    m_ref[...] = jnp.full_like(m_ref, masked_score)
    l_ref[...] = jnp.zeros_like(l_ref)
    acc_ref[...] = jnp.zeros_like(acc_ref)
    take, chunks = from_refs(kv_refs)
    attend_rows(turned, take, chunks, m_ref, l_ref, acc_ref)


def next_kernel(count, turned, m_in, l_in, acc_in, *refs):
    kv_refs = refs[:count]
    m_ref, l_ref, acc_ref = refs[count:]
    m_ref[...] = m_in[...]
    l_ref[...] = l_in[...]
    acc_ref[...] = acc_in[...]
    take, chunks = from_refs(kv_refs)
    attend_rows(turned, take, chunks, m_ref, l_ref, acc_ref)


def attention_params(rows, keys):
    return dict(
        compiler_params=pltpu.CompilerParams(vmem_limit_bytes=36 * MIB),
        cost_estimate=pl.CostEstimate(
            flops=1024 * rows * keys, bytes_accessed=512 * keys, transcendentals=rows * keys
        ),
    )


def state_shapes(rows):
    return [
        jax.ShapeDtypeStruct((1, rows), jnp.float32),
        jax.ShapeDtypeStruct((1, rows), jnp.float32),
        jax.ShapeDtypeStruct((128, rows), jnp.float32),
    ]


def attend_first(heads, blocks, rows, scale):
    vmem = pl.BlockSpec(memory_space=pltpu.VMEM)
    return pl.pallas_call(
        functools.partial(first_kernel, scale, len(blocks)),
        in_specs=[vmem] * (len(heads) + len(blocks)),
        out_specs=[vmem] * 4,
        out_shape=[jax.ShapeDtypeStruct((256, rows), jnp.bfloat16)] + state_shapes(rows),
        **attention_params(rows, len(blocks) * blocks[0].shape[0]),
    )(*heads, *blocks)


def attend_next(state, blocks):
    turned, *rest = state
    rows = turned.shape[1]
    vmem = pl.BlockSpec(memory_space=pltpu.VMEM)
    rest = pl.pallas_call(
        functools.partial(next_kernel, len(blocks)),
        in_specs=[vmem] * (4 + len(blocks)),
        out_specs=[vmem] * 3,
        out_shape=state_shapes(rows),
        **attention_params(rows, len(blocks) * blocks[0].shape[0]),
    )(turned, *rest, *blocks)
    return [turned, *rest]


def span_kernel(tokens, span_ref, *refs):
    states = (refs[:4], refs[4:8])
    kv_ref, o_ref, turned, m_ref, l_ref, acc_ref = refs[8:]
    rows = refs[1].shape[1]
    for half, state in enumerate(states):
        cols = slice(half * rows, (half + 1) * rows)
        for to_ref, from_ref in zip((turned, m_ref, l_ref, acc_ref), state):
            to_ref[:, cols] = from_ref[...]
    first_query = span_ref[0] * tokens
    last = first_query // key_chunk

    def taker(chunk):
        def take(k, which):
            first = pl.multiple_of((chunk + k) * key_chunk, key_chunk)
            return kv_ref[pl.ds(first, key_chunk), which * 128 : (which + 1) * 128]

        return take

    @pl.when(last >= 2)
    def _():
        attend_rows(turned, taker(0), 2, m_ref, l_ref, acc_ref)

    @pl.when(last % 2 == 1)
    def _():
        attend_rows(turned, taker(last - 1), 1, m_ref, l_ref, acc_ref)

    key = lax.broadcasted_iota(jnp.int32, (key_chunk, 1), 0) + (last * key_chunk - first_query)

    def allowed(c):
        token = lax.broadcasted_iota(jnp.int32, (1, query_chunk), 1) % tokens
        return key <= token

    attend_rows(turned, taker(last), 1, m_ref, l_ref, acc_ref, allowed)
    inverse = 1.0 / l_ref[...]
    for j in range(acc_ref.shape[1] // 128):
        cols = slice(j * 128, (j + 1) * 128)
        o_ref[:, cols] = (acc_ref[:, cols] * inverse[:, cols]).T.astype(jnp.bfloat16)


def attend_span(span, first_state, second_state, key_rows, tokens):
    rows = first_state[0].shape[1]
    vmem = pl.BlockSpec(memory_space=pltpu.VMEM)
    smem = pl.BlockSpec(memory_space=pltpu.SMEM)
    return pl.pallas_call(
        functools.partial(span_kernel, tokens),
        in_specs=[smem] + [vmem] * 9,
        out_specs=vmem,
        out_shape=jax.ShapeDtypeStruct((tokens, 2 * rows * 128 // tokens), jnp.bfloat16),
        scratch_shapes=[
            pltpu.VMEM((256, 2 * rows), jnp.bfloat16),
            pltpu.VMEM((1, 2 * rows), jnp.float32),
            pltpu.VMEM((1, 2 * rows), jnp.float32),
            pltpu.VMEM((128, 2 * rows), jnp.float32),
        ],
        **attention_params(2 * rows, key_rows.shape[0]),
    )(span, *first_state, *second_state, key_rows)


def shift(block, axis, by, size=4):
    return lax.ppermute(block, axis, [(i, (i + by) % size) for i in range(size)])


def ring(block, axis):
    return [shift(block, axis, by) for by in (1, -1, 2)]


def body(residual_in, expert_hidden, w_down, routes, gates, norm_gain, w_qkv, cache_kv):
    x, zh, y = lax.axis_index("x"), lax.axis_index("zh"), lax.axis_index("y")
    zl, core = lax.axis_index("zl"), lax.axis_index("c")
    seq_index = lax.axis_index(seq_axes)
    slot_cap = expert_hidden.shape[2]
    head_dim = cache_kv.shape[3]
    token_count, per_token = routes.shape
    seq_size = lax.axis_size(seq_axes)
    cache_length = cache_kv.shape[0] * seq_size
    tok_seq = token_count * lax.axis_size(head_axes)

    weight = lax.all_gather(w_qkv[:, 0, :], ("x", "y"), axis=0, tiled=True)

    own_cache = cache_kv.reshape(-1, 2 * head_dim)
    partner_cache = shift(own_cache, "zh", 1, 2)
    hidden = expert_hidden[0].reshape(-1, expert_hidden.shape[3])
    produced = expert_rows(hidden, w_down[0])
    returned = lax.all_to_all(produced, token_axes, split_axis=0, concat_axis=0, tiled=True)
    first_ring = [own_cache] + ring(own_cache, "x")
    second_ring = [partner_cache] + ring(partner_cache, "y")

    row_index = (routes * slot_cap + slot_numbers(routes)).reshape(-1)
    stream, planes = combine(
        row_index,
        gates.reshape(-1),
        returned.reshape(-1, column_parts, returned.shape[1]),
        residual_in,
        norm_gain[None, :],
    )
    near = lax.all_to_all(planes, ("zh", "zl"), split_axis=0, concat_axis=0, tiled=True)
    near, first_ring, second_ring = lax.optimization_barrier((near, first_ring, second_ring))
    far = shift(near, "c", 1, 2)
    first_cache = jnp.concatenate(first_ring, axis=0)
    second_cache = jnp.concatenate(second_ring, axis=0)
    first_others = ring(first_cache, "y")
    second_others = ring(second_cache, "x")
    places = jnp.stack(
        [
            jnp.where(zh == z // 2, 0, tok_seq) + z % 2 * 2 * token_count + c * token_count
            for c in (core, 1 - core)
            for z in range(4)
        ]
    )

    half_dim = head_dim // 2
    inverse = rope_base ** (-2.0 * jnp.arange(half_dim, dtype=jnp.float32) / head_dim)
    span_index = seq_index * tok_seq + jnp.arange(tok_seq, dtype=jnp.int32)
    angles = (span_index + cache_length).astype(jnp.float32)[:, None] * inverse[None, :]
    cosine = jnp.cos(angles)
    sine = jnp.sin(angles)
    cosine = jnp.concatenate([cosine, cosine], axis=1)
    sine = jnp.concatenate([-sine, sine], axis=1)

    half = (w_qkv.shape[2] - 2 * head_dim) // 2
    first_kept, first_sent = project(
        places, [near, far], weight, ((0, half), (2 * half, 2 * head_dim))
    )
    first_received = shift(first_sent, "zh", 1, 2)
    second_kept, second_sent = project(places, [near, far], weight, ((half, half),))
    second_received = shift(second_sent, "zh", 1, 2)
    span_kv = new_rows(first_kept, first_received, cosine, sine, seq_size)
    key_rows = lax.all_to_all(span_kv, seq_axes, split_axis=0, concat_axis=0, tiled=True)

    scale = head_dim ** (-0.5) * log2_e
    rows = tok_seq * half // head_dim
    first_heads = (first_kept, first_received, cosine, sine)
    second_heads = (second_kept, second_received, cosine, sine)
    first_part = [first_cache, second_cache] + first_others[:2]
    second_part = second_others + first_others[2:]
    first_state = attend_first(first_heads, first_part, rows, scale)
    second_state = attend_first(second_heads, first_part, rows, scale)
    first_state = attend_next(first_state, second_part)
    second_state = attend_next(second_state, second_part)
    attended = attend_span(seq_index[None], first_state, second_state, key_rows, tok_seq)
    return (stream, attended[:, None, :])


def solution(mesh):
    fine = Mesh(mesh.devices.reshape(4, 2, 4, 2, 2), token_axes)
    in_specs = (
        P(token_axes, None),
        P(token_axes, None, None, None),
        P(token_axes, None, None),
        P(token_axes, None),
        P(token_axes, None),
        P(),
        P(seq_axes, head_axes, None),
        P(seq_axes, head_axes, None, None),
    )
    out_specs = (P(token_axes, None), P(seq_axes, head_axes, None))
    return jax.shard_map(body, mesh=fine, in_specs=in_specs, out_specs=out_specs, check_vma=False)
```
